128 devices in a mesh: chain: 8 (over x, core), band: 16 (over z, y).
Axes of the slice: x: 4, y: 4, z: 4, core: 2. Of those that a mesh axis runs over, the one named last changes fastest.
Arguments:
- diag_inverse: float32 [16384, 2048], P(('chain', 'band'))
- coupling: float32 [16384, 2048], P('chain', 'band'), may hold values from -0.09375 to 0.09375
- elem_stiff: float32 [24, 24, 65536], P(None, None, ('chain', 'band')), may hold values from -6 to 6
- elem_mass: float32 [24, 24, 65536], P(None, None, ('chain', 'band')), may hold values from -6 to 6
- elem_dofs: int32 [24, 65536], P(None, ('chain', 'band')), may hold values from 0 to 2047
- elem_slab: int32 [65536, 1], P(('chain', 'band')), may hold values from 0 to 7; in each aligned block of 512 rows (0 to 511, 512 to 1023, ...) at most 128 rows name the same one
- elem_var: int32 [65536], P(('chain', 'band')), may hold values from 0 to 191
- mode: float32 [16384], P(('chain', 'band')), may hold values from -0.4 to 0.4
- mass_mode: float32 [16384], P('chain'), may hold values from -1.2 to 1.2
- eigenvalue: float32 [1], replicated, may hold values from 0.5 to 2
Outputs:
- eigvec_slope: float32 [192, 16384], P(None, ('chain', 'band'))
- eigval_slope: float32 [192], replicated
The draws below stay inside these ranges and needn't reach their ends.
Inputs may be any that keep to these rules, and one draw needn't show every extreme that they name: `elem_slab`: within the rows of one device no slab is named by more than 128 elements, a bound that some block reaches.
All inputs are finite; a program needn't handle non-finite values.
Results may differ from the reference program's by a relative error of at most 0.00014.
Values sent between devices are 32-bit elements; how exact they have to be, the bound alone decides.
A program may use at most 64 MiB of HBM per device.

```python
import math
import jax
import jax.numpy as jnp
import numpy as np
from jax import lax

B = 2048
ED = 24
VARS = 192
EL_DEV = 512
NDOF = 16384
ELEMS = 65536
CAP = 128
N_CHAIN = 8


def draw_diag_inverse(key, part):
    first_key, second_key = jax.random.split(jax.random.fold_in(key, 11))
    spread = jax.random.normal(first_key, (NDOF, B), jnp.float32) * (0.3 / B ** 0.5)
    diagonal = jax.random.uniform(second_key, (NDOF, 1), jnp.float32, minval=0.75, maxval=1.5)
    on_diagonal = jnp.arange(NDOF)[:, None] % B == jnp.arange(B)[None, :]
    return jnp.where(on_diagonal, diagonal, spread)


def with_ends(entries, stream_key, smallest, high):
    index_at = [jax.random.randint(jax.random.fold_in(stream_key, axis), (), 0, length) for axis, length in enumerate(entries.shape)]
    main_axis = entries.shape.index(max(entries.shape))
    beside = index_at[:main_axis] + [(index_at[main_axis] + 1) % entries.shape[main_axis]] + index_at[main_axis + 1:]
    return entries.at[tuple(index_at)].set(smallest).at[tuple(beside)].set(high)


def shard_levels(key, extent, cuts, smallest, high):
    def one(dim, blocks):
        draws = jax.random.uniform(jax.random.fold_in(jax.random.fold_in(key, 6), dim), (blocks,), jnp.float32, smallest / len(cuts), high / len(cuts))
        return jnp.repeat(jnp.exp(draws), extent[dim] // blocks).reshape((-1,) + (1,) * (len(extent) - dim - 1))

    level = one(*cuts[0])
    for cut in cuts[1:]:
        level = level * one(*cut)
    return level


def deal_out(key, own, number, rows, amount, top, bound, lean):
    order = jax.random.permutation(key, amount)
    packed, common = portions_of(amount, rows * top, bound, lean, True), portions_of(amount, rows * top, bound, lean, False)
    places = jnp.arange(amount)

    def named(lengths, offset_by):
        used = int((lengths > 0).sum())
        fixed = max(1, used // 4)
        shifted = fixed + (places - fixed + offset_by * (used - fixed)) % max(1, amount - fixed)
        return jnp.zeros((amount,), jnp.int32).at[order[jnp.where(places < fixed, places, shifted)]].set(jnp.asarray(lengths, jnp.int32))

    lengths = jnp.where(number % 4 == 0, named(packed, number // 4), named(common, number - number // 4 - 1))
    mixed = jax.random.permutation(jax.random.fold_in(own, 3), amount)
    giver, taker = mixed[0:amount // 2 * 2:2], mixed[1:amount // 2 * 2:2]
    room = jnp.minimum(lengths[giver] - 1, bound - lengths[taker]) // 2
    room = jnp.where((giver == order[0]) | (taker == order[0]) | (lengths[taker] == 0), 0, jnp.maximum(room, 0))
    shifted = jax.random.randint(jax.random.fold_in(own, 4), (amount // 2,), 0, 1 << 20) % (room + 1)
    lengths = lengths.at[giver].add(-shifted).at[taker].add(shifted)
    members = jnp.searchsorted(jnp.cumsum(lengths), jnp.arange(rows * top), side="right").astype(jnp.int32)
    listing = members.reshape(top, rows).T
    listing = listing[jax.random.permutation(jax.random.fold_in(own, 1), rows)]
    offset_by = jax.random.randint(jax.random.fold_in(own, 2), (rows, 1), 0, top)
    return jnp.take_along_axis(listing, (jnp.arange(top)[None, :] + offset_by) % top, axis=1)


def portions_of(number_of, total, reach, lean, full):
    weights = [(1 << 20) // math.isqrt(rank ** lean) + 1 for rank in range(1, number_of + 1)]
    largest = reach if full else min(reach, max(-(-total // number_of), total * weights[0] // sum(weights)))
    least = 1 if total - largest >= number_of - 1 else 0
    given, surplus = [largest] + [least] * (number_of - 1), total - largest - least * (number_of - 1)
    while surplus > 0:
        free = [i for i in range(1, number_of) if given[i] < largest] or [i for i in range(1, number_of) if given[i] < reach]
        whole, left = sum([weights[i] for i in free]), surplus
        for i in free:
            addition = min(reach - given[i], max(1, left * weights[i] // whole), surplus)
            given[i] = given[i] + addition
            surplus = surplus - addition
    return np.array(given)


def centred(key, extent, scale, most, shards=(), kind=jnp.bfloat16):
    loudness = shard_levels(key, extent, shards, -0.22, 0.18) if shards else 1.0
    values = jax.random.normal(key, extent, jnp.float32) * scale * loudness
    return jnp.minimum(jnp.maximum(values, -most), most).astype(kind)


def setup_inputs(seed: int = 0) -> dict:
    key_list = jax.random.split(jax.random.key(seed), 11)
    diag_inverse = draw_diag_inverse(jax.random.fold_in(key_list[10], 71), 0)
    coupling = centred(key_list[1], (NDOF, B), (2 * B) ** -0.5, 0.09375, ((0, 8), (1, 16)), jnp.float32)
    elem_stiff = centred(key_list[2], (ED, ED, ELEMS), 1.0, 6.0, ((2, 128),), jnp.float32)
    elem_mass = centred(key_list[3], (ED, ED, ELEMS), 1.0, 6.0, ((2, 128),), jnp.float32)
    elem_dofs = with_ends(jax.random.randint(key_list[4], (ED, ELEMS), 0, B), jax.random.fold_in(key_list[4], 1), 0, B - 1).astype(jnp.int32)
    elem_slab_keys = jax.random.split(jax.random.fold_in(key_list[5], 1), ELEMS // EL_DEV)
    elem_slab_turns = jax.random.permutation(jax.random.fold_in(key_list[5], 3), ELEMS // EL_DEV)
    elem_slab = jax.vmap(lambda own, number: deal_out(jax.random.fold_in(key_list[5], 2), own, number, EL_DEV, N_CHAIN, 1, CAP, 2))(elem_slab_keys, elem_slab_turns).reshape((ELEMS, 1))
    elem_var = with_ends(jax.random.randint(key_list[6], (ELEMS,), 0, VARS), jax.random.fold_in(key_list[6], 1), 0, VARS - 1).astype(jnp.int32)
    mode = centred(key_list[7], (NDOF,), 0.05, 0.4, ((0, 128),), jnp.float32)
    mass_mode = centred(key_list[8], (NDOF,), 0.15, 1.2, ((0, 8),), jnp.float32)
    eigenvalue = jnp.clip(jax.random.uniform(key_list[9], (1,), jnp.float32, 0.5, 2.0), 0.5, 2.0)
    return {"diag_inverse": diag_inverse, "coupling": coupling, "elem_stiff": elem_stiff, "elem_mass": elem_mass, "elem_dofs": elem_dofs, "elem_slab": elem_slab, "elem_var": elem_var, "mode": mode, "mass_mode": mass_mode, "eigenvalue": eigenvalue}


def reference(diag_inverse, coupling, elem_stiff, elem_mass, elem_dofs, elem_slab, elem_var, mode, mass_mode, eigenvalue):
    highest = lax.Precision.HIGHEST
    eigen_val = eigenvalue[0]
    dof_index = (elem_slab[:, 0][None, :] * B + elem_dofs).astype(jnp.int32)
    mode_at = mode[dof_index]
    operator = elem_stiff - eigen_val * elem_mass
    loads = -jnp.einsum("ije,je->ie", operator, mode_at, precision=highest)
    quadratic = -jnp.sum(mode_at * loads, axis=0)
    eigval_slope = jax.ops.segment_sum(quadratic, elem_var, num_segments=VARS)
    var_rows = jnp.broadcast_to(elem_var[None, :], dof_index.shape).astype(jnp.int32)
    rhs = jnp.zeros((VARS, NDOF), mode.dtype).at[var_rows, dof_index].add(loads)
    rhs = rhs + eigval_slope[:, None] * mass_mode[None, :]
    solved = []
    previous = jnp.zeros((VARS, B), mode.dtype)
    for slab_no in range(N_CHAIN):
        lower = slab_no * B
        coupled = rhs[:, lower:lower + B]
        if slab_no > 0:
            coupled = coupled - jnp.dot(previous, coupling[lower:lower + B].T, precision=highest)
        previous = jnp.dot(coupled, diag_inverse[lower:lower + B].T, precision=highest)
        solved.append(previous)
    results = [None] * N_CHAIN
    following = jnp.zeros((VARS, B), mode.dtype)
    for slab_no in range(N_CHAIN - 1, -1, -1):
        lower = slab_no * B
        remain = solved[slab_no]
        if slab_no < N_CHAIN - 1:
            upper = lower + B
            remain = remain - jnp.dot(following, coupling[upper:upper + B], precision=highest)
        following = jnp.dot(remain, diag_inverse[lower:lower + B], precision=highest)
        results[slab_no] = following
    eigvec_slope = jnp.concatenate(results, axis=1)
    return eigvec_slope, eigval_slope
```

```python
import functools

import jax
import jax.numpy as jnp
from jax import lax
from jax.experimental import pallas as pl
from jax.experimental.pallas import tpu as pltpu
from jax.sharding import PartitionSpec as P

MESH = pl.DeviceIdType.MESH
F32 = jnp.float32
BF16 = jnp.bfloat16
VARS = 192


def split2(x):
    high = x.astype(BF16)
    return high, (x - high.astype(F32)).astype(BF16)


def stacked_rows(x):
    high = x.astype(BF16).astype(F32)
    return jnp.concatenate([high, x - high], axis=0).astype(BF16)


def sweep_kernel(nc, nb, *refs):
    diag_refs, coup_refs = refs[:nc], refs[nc : 2 * nc]
    (rhs_ref, out_ref, dbuf, cbuf, dsplit, csplit, part, slots, piece, full, ybuf, xbuf,
     load_sem, rs_send, rs_recv, ag_send, ag_recv, out_send, out_recv) = refs[2 * nc :]
    me, band = lax.axis_index("chain"), lax.axis_index("band")
    x_len = nc // 2
    my_x, my_core = me // 2, lax.rem(me, 2)
    rows, width = rhs_ref.shape[1], rhs_ref.shape[2]
    cols = width // nb

    def at_band(b):
        return pl.ds(pl.multiple_of(b * cols, cols), cols)

    for i in range(nc):
        slab = 2 * lax.rem(my_x - i // 2 + x_len, x_len) + lax.rem(my_core + i % 2, 2)
        pltpu.make_async_copy(diag_refs[i], dbuf.at[slab], load_sem.at[0, slab]).start()
        pltpu.make_async_copy(coup_refs[i], cbuf.at[slab], load_sem.at[1, slab]).start()

    barrier = pltpu.get_barrier_semaphore()
    for r in range(1, nb):
        pl.semaphore_signal(barrier, inc=1, device_id=(me, lax.rem(band + r, nb)), device_id_type=MESH)
    for r in range(1, nc):
        pl.semaphore_signal(barrier, inc=1, device_id=(lax.rem(me + r, nc), band), device_id_type=MESH)
    pl.semaphore_wait(barrier, nb + nc - 2)

    def rs_copy(r):
        to = lax.rem(band + r, nb)
        return pltpu.make_async_remote_copy(
            src_ref=part.at[:, at_band(to)], dst_ref=slots.at[r],
            send_sem=rs_send.at[r], recv_sem=rs_recv.at[r], device_id=(me, to), device_id_type=MESH)

    def ag_copy(r):
        to = lax.rem(band + r, nb)
        return pltpu.make_async_remote_copy(
            src_ref=piece, dst_ref=full.at[:, at_band(band)],
            send_sem=ag_send.at[r], recv_sem=ag_recv.at[r], device_id=(me, to), device_id_type=MESH)

    def ag_arrival(r):
        source = lax.rem(band - r + nb, nb)
        return pltpu.make_async_remote_copy(
            src_ref=piece, dst_ref=full.at[:, at_band(source)],
            send_sem=ag_send.at[r], recv_sem=ag_recv.at[r], device_id=(me, source), device_id_type=MESH)

    def reduce_start():
        for r in range(1, nb):
            rs_copy(r).start()

    def reduce_end():
        total = part[:, at_band(band)]
        for r in range(1, nb):
            rs_copy(r).wait_recv()
            total = total + slots[r]
        for r in range(1, nb):
            rs_copy(r).wait_send()
        return total

    def gather_start(value):
        piece[...] = value
        for r in range(1, nb):
            ag_copy(r).start()
        full[:, at_band(band)] = value

    def gather_end():
        for r in range(1, nb):
            ag_arrival(r).wait_recv()
        for r in range(1, nb):
            ag_copy(r).wait_send()

    def split_diag(k):
        pltpu.make_async_copy(diag_refs[0], dbuf.at[k], load_sem.at[0, k]).wait()
        high, low = split2(dbuf[k])
        dsplit[k, 0:cols, :] = high
        dsplit[k, cols : 2 * cols, :] = low

    def split_coup(k):
        pltpu.make_async_copy(coup_refs[0], cbuf.at[k], load_sem.at[1, k]).wait()
        high, low = split2(cbuf[k])
        csplit[k, :, 0:cols] = high
        csplit[k, :, cols : 2 * cols] = low

    nt = (((1,), (1,)), ((), ()))
    nn = (((1,), (0,)), ((), ()))

    def narrow(value, weights, dims):
        wide = lax.dot_general(stacked_rows(value), weights, dims, preferred_element_type=F32)
        return (wide[:rows, :cols] + wide[:rows, cols:]) + (wide[rows:, :cols] + wide[rows:, cols:])

    def spread(value, weights, dims):
        both = stacked_rows(value)
        both = jnp.concatenate([both, both], axis=1)
        wide = lax.dot_general(both, weights, dims, preferred_element_type=F32)
        return wide[:rows] + wide[rows:]

    part[...] = rhs_ref[0]

    def forward(k, carry):
        reduce_start()
        split_diag(k)
        gather_start(reduce_end())

        @pl.when(k + 1 < nc)
        def _():
            split_coup(k + 1)

        gather_end()
        solved = narrow(full[...], dsplit[k], nt)
        ybuf[k] = solved

        @pl.when(k + 1 < nc)
        def _():
            part[...] = rhs_ref[k + 1] - spread(solved, csplit[k + 1], nt)

        return carry

    lax.fori_loop(0, nc, forward, 0)
    split_coup(0)

    def out_copy(k, source):
        return pltpu.make_async_remote_copy(
            src_ref=xbuf.at[k], dst_ref=out_ref.at[pl.ds(pl.multiple_of(source * rows, 8), rows), :],
            send_sem=out_send.at[k], recv_sem=out_recv.at[source], device_id=(k, band), device_id_type=MESH)

    def backward(step, coupled):
        k = nc - 1 - step
        part[...] = spread(ybuf[k] - coupled, dsplit[k], nn)
        reduce_start()
        total = reduce_end()
        gather_start(total)
        xbuf[k] = total

        @pl.when(k != me)
        def _():
            out_copy(k, me).start()

        @pl.when(k == me)
        def _():
            out_ref[pl.ds(pl.multiple_of(me * rows, 8), rows), :] = total

        gather_end()
        return narrow(full[...], csplit[k], nn)

    lax.fori_loop(0, nc, backward, jnp.zeros((rows, cols), F32))

    for r in range(1, nc):
        out_copy(lax.rem(me + r, nc), me).wait_send()
        out_copy(me, lax.rem(me + r, nc)).wait_recv()


def sweep(diag_blocks, coup_blocks, rhs, nc, nb):
    rows, width = rhs.shape[1], rhs.shape[2]
    cols = width // nb
    flops = 2 * nc * 2 * 2 * 2 * (2 * rows) * width * (2 * cols) // 2
    return pl.pallas_call(
        functools.partial(sweep_kernel, nc, nb),
        out_shape=jax.ShapeDtypeStruct((nc * rows, cols), F32),
        in_specs=[pl.BlockSpec(memory_space=pl.ANY)] * (2 * nc) + [pl.BlockSpec(memory_space=pltpu.VMEM)],
        out_specs=pl.BlockSpec(memory_space=pltpu.VMEM),
        scratch_shapes=[
            pltpu.VMEM((nc, cols, width), F32),
            pltpu.VMEM((nc, width, cols), F32),
            pltpu.VMEM((nc, 2 * cols, width), BF16),
            pltpu.VMEM((nc, width, 2 * cols), BF16),
            pltpu.VMEM((rows, width), F32),
            pltpu.VMEM((nb, rows, cols), F32),
            pltpu.VMEM((rows, cols), F32),
            pltpu.VMEM((rows, width), F32),
            pltpu.VMEM((nc, rows, cols), F32),
            pltpu.VMEM((nc, rows, cols), F32),
            pltpu.SemaphoreType.DMA((2, nc)),
            pltpu.SemaphoreType.DMA((nb,)),
            pltpu.SemaphoreType.DMA((nb,)),
            pltpu.SemaphoreType.DMA((nb,)),
            pltpu.SemaphoreType.DMA((nb,)),
            pltpu.SemaphoreType.DMA((nc,)),
            pltpu.SemaphoreType.DMA((nc,)),
        ],
        compiler_params=pltpu.CompilerParams(collective_id=0, has_side_effects=True, vmem_limit_bytes=50 * 1024 * 1024),
        cost_estimate=pl.CostEstimate(flops=flops, bytes_accessed=4 * nc * 2 * cols * width, transcendentals=0),
        name="sweep",
    )(*diag_blocks, *coup_blocks, rhs)


def replicate_chain(block, nc):
    x_len = nc // 2
    found = []
    for by in range(x_len):
        moved = block
        if by:
            pairs = [(2 * x + core, 2 * ((x + by) % x_len) + core) for x in range(x_len) for core in range(2)]
            moved = lax.ppermute(block, "chain", pairs)
        found.append(moved)
    out = []
    swap = [(2 * x + core, 2 * x + 1 - core) for x in range(x_len) for core in range(2)]
    for moved in found:
        out += [moved, lax.ppermute(moved, "chain", swap)]
    return out
def three_way(x):
    high = x.astype(BF16).astype(F32)
    middle = (x - high).astype(BF16).astype(F32)
    return high, middle, x - high - middle


def loads_kernel(nc, nvars, lam_ref, table_ref, stiff_ref, mass_ref, dofs_ref, slab_ref, var_ref,
                 send_ref, slope_ref, mode_at, loads):
    ed, count = dofs_ref.shape
    lanes = table_ref.shape[1]
    cap = send_ref.shape[2]
    per_slab = table_ref.shape[0] // nc
    lam = lam_ref[0]
    dofs, slab, var = dofs_ref[...], slab_ref[...], var_ref[...]
    row_of = slab * per_slab + lax.shift_right_logical(dofs, 7)
    lane_of = jnp.bitwise_and(dofs, lanes - 1)
    chunks = count // lanes

    def look(step, found):
        found = list(found)
        for inner in range(8):
            r = step * 8 + inner
            row = jnp.broadcast_to(table_ref[pl.ds(r, 1), :], (ed, lanes))
            for c in range(chunks):
                at = slice(c * lanes, (c + 1) * lanes)
                taken = jnp.take_along_axis(row, lane_of[:, at], axis=1, mode="promise_in_bounds")
                found[c] = jnp.where(row_of[:, at] == r, taken, found[c])
        return tuple(found)

    found = lax.fori_loop(0, table_ref.shape[0] // 8, look, (jnp.zeros((ed, lanes), F32),) * chunks)
    for c in range(chunks):
        mode_at[:, c * lanes : (c + 1) * lanes] = found[c]
    modes = mode_at[...]
    for i in range(ed):
        operator = stiff_ref[i] - lam * mass_ref[i]
        loads[i : i + 1, :] = -jnp.sum(operator * modes, axis=0, keepdims=True)
    values = loads[...]
    quadratic = -jnp.sum(modes * values, axis=0, keepdims=True)
    matches = (lax.broadcasted_iota(jnp.int32, (nvars, count), 0) == var).astype(F32).astype(BF16)
    terms = jnp.concatenate(list(three_way(quadratic)) + [jnp.zeros((5, count), F32)], axis=0).astype(BF16)
    nt = (((1,), (1,)), ((), ()))
    sums = lax.dot_general(terms, matches, nt, preferred_element_type=F32)
    slope_ref[...] = jnp.sum(sums, axis=0, keepdims=True)
    merged = jnp.zeros((ed, count), F32)
    for i in range(ed):
        merged = merged + jnp.where(dofs == dofs[i : i + 1, :], values[i : i + 1, :], 0.0)
    onehot = (lax.broadcasted_iota(jnp.int32, (nc, count), 0) == slab).astype(F32)
    earlier = lax.broadcasted_iota(jnp.int32, (count, count), 0) < lax.broadcasted_iota(jnp.int32, (count, count), 1)
    rank_all = jnp.dot(onehot.astype(BF16), earlier.astype(F32).astype(BF16), preferred_element_type=F32)
    rank = jnp.sum(onehot * rank_all, axis=0, keepdims=True).astype(jnp.int32)
    slot = slab * cap + rank
    high, middle, low = three_way(merged)
    coarse = lax.shift_right_logical(dofs, 4).astype(F32)
    fine = jnp.bitwise_and(dofs, 15).astype(F32)
    var_rows = jnp.concatenate([var.astype(F32), jnp.zeros((7, count), F32)], axis=0)
    data = jnp.concatenate([high, middle, low, coarse, fine, var_rows], axis=0).astype(BF16)
    for k in range(nc):
        place = (lax.broadcasted_iota(jnp.int32, (cap, count), 0) + k * cap == slot).astype(F32).astype(BF16)
        packed = lax.dot_general(data, place, nt, preferred_element_type=F32)
        send_ref[k, 0:ed, :] = (packed[0:ed] + packed[ed : 2 * ed]) + packed[2 * ed : 3 * ed]
        send_ref[k, ed : 2 * ed, :] = packed[3 * ed : 4 * ed] * 16.0 + packed[4 * ed : 5 * ed]
        send_ref[k, 2 * ed : 2 * ed + 8, :] = packed[5 * ed : 5 * ed + 8]


def scatter_kernel(nc, got_ref, slope_ref, mass_ref, rhs_ref, spread_ref):
    width = mass_ref.shape[1]
    nvars = slope_ref.shape[0]
    cap = got_ref.shape[2]
    ed = (got_ref.shape[1] - 8) // 2
    block = 256
    rows = 128
    base = lax.broadcasted_iota(jnp.int32, (rows, cap), 0)
    variable = lax.broadcasted_iota(jnp.int32, (nvars, cap), 0)
    matches = [(variable == got_ref[s, 2 * ed : 2 * ed + 1, :].astype(jnp.int32)).astype(F32).astype(BF16) for s in range(nc)]
    matches = jnp.concatenate(matches + matches, axis=1)
    nt = (((1,), (1,)), ((), ()))

    def one_block(n, carry):
        def one_source(s, inner):
            values = got_ref[s, 0:ed, :]
            dofs = got_ref[s, ed : 2 * ed, :].astype(jnp.int32) - n * block
            for half in range(block // rows):
                total = jnp.zeros((rows, cap), F32)
                for i in range(ed):
                    hit = base == dofs[i : i + 1, :] - half * rows
                    total = jnp.where(hit, values[i : i + 1, :], total)
                high = total.astype(BF16)
                at = pl.ds(pl.multiple_of(s * cap, cap), cap)
                spread_ref[half * rows : (half + 1) * rows, at] = high
                at = pl.ds(pl.multiple_of((s + nc) * cap, cap), cap)
                spread_ref[half * rows : (half + 1) * rows, at] = (total - high.astype(F32)).astype(BF16)
            return inner

        lax.fori_loop(0, nc, one_source, 0)
        at = pl.ds(pl.multiple_of(n * block, block), block)
        summed = lax.dot_general(matches, spread_ref[...], nt, preferred_element_type=F32)
        rhs_ref[:, at] = summed + slope_ref[...] * mass_ref[:, at]
        return carry

    lax.fori_loop(0, width // block, one_block, 0)


def on_device(nc, nb, diag_inverse, coupling, elem_stiff, elem_mass, elem_dofs, elem_slab, elem_var, mode, mass_mode, eigenvalue):
    band = lax.axis_index("band")
    cols, width = diag_inverse.shape
    ed, count = elem_dofs.shape
    cap = count // 4
    everyone = nc * nb
    vmem = pl.BlockSpec(memory_space=pltpu.VMEM)
    diag_blocks = replicate_chain(diag_inverse, nc)
    coup_blocks = replicate_chain(coupling, nc)
    table = lax.all_to_all(jnp.broadcast_to(mode[None, :], (everyone, cols)), ("chain", "band"), 0, 0, tiled=True)
    send, slope = pl.pallas_call(
        functools.partial(loads_kernel, nc, VARS),
        out_shape=(jax.ShapeDtypeStruct((nc, 2 * ed + 8, cap), F32), jax.ShapeDtypeStruct((1, VARS), F32)),
        in_specs=[pl.BlockSpec(memory_space=pltpu.SMEM)] + [vmem] * 6,
        out_specs=(vmem, vmem),
        scratch_shapes=[pltpu.VMEM((ed, count), F32), pltpu.VMEM((ed, count), F32)],
        compiler_params=pltpu.CompilerParams(vmem_limit_bytes=30 * 1024 * 1024),
        cost_estimate=pl.CostEstimate(flops=2 * 10**9, bytes_accessed=10**7, transcendentals=0),
        name="loads",
    )(eigenvalue, table, elem_stiff, elem_mass, elem_dofs, elem_slab.reshape(1, count), elem_var.reshape(1, count))
    got = lax.all_to_all(send, "chain", 0, 0, tiled=True)
    slopes = lax.all_to_all(jnp.broadcast_to(slope, (everyone, VARS)), ("chain", "band"), 0, 0, tiled=True)
    eigval_slope = jnp.sum(slopes, axis=0)
    own = lax.broadcasted_iota(jnp.int32, (1, width), 1) // cols == band
    own_mass = jnp.where(own, mass_mode[None, :], 0.0)
    rhs = pl.pallas_call(
        functools.partial(scatter_kernel, nc),
        out_shape=jax.ShapeDtypeStruct((VARS, width), F32),
        in_specs=[vmem] * 3,
        out_specs=vmem,
        scratch_shapes=[pltpu.VMEM((256, 2 * nc * cap), BF16)],
        compiler_params=pltpu.CompilerParams(vmem_limit_bytes=30 * 1024 * 1024),
        cost_estimate=pl.CostEstimate(flops=5 * 10**9, bytes_accessed=10**7, transcendentals=0),
        name="scatter",
    )(got, eigval_slope[:, None], own_mass)
    rhs = lax.all_to_all(rhs.reshape(nc, VARS // nc, width), "chain", 0, 0, tiled=True)
    return sweep(diag_blocks, coup_blocks, rhs, nc, nb), eigval_slope


def solution(mesh):
    nc, nb = mesh.shape["chain"], mesh.shape["band"]
    in_specs = (
        P(("chain", "band"), None),
        P("chain", "band"),
        P(None, None, ("chain", "band")),
        P(None, None, ("chain", "band")),
        P(None, ("chain", "band")),
        P(("chain", "band"), None),
        P(("chain", "band")),
        P(("chain", "band")),
        P("chain"),
        P(),
    )
    out_specs = (P(None, ("chain", "band")), P())
    return jax.shard_map(functools.partial(on_device, nc, nb), mesh=mesh, in_specs=in_specs, out_specs=out_specs, check_vma=False)
```

```python
import functools

import jax
import jax.numpy as jnp
from jax import lax
from jax.experimental import pallas as pl
from jax.experimental.pallas import tpu as pltpu
from jax.sharding import PartitionSpec as P

MESH = pl.DeviceIdType.MESH
F32 = jnp.float32
BF16 = jnp.bfloat16
VARS = 192


def split2(x):
    high = x.astype(BF16)
    return high, (x - high.astype(F32)).astype(BF16)


def stacked_rows(x):
    high = x.astype(BF16).astype(F32)
    return jnp.concatenate([high, x - high], axis=0).astype(BF16)


def three_way(x):
    high = x.astype(BF16).astype(F32)
    middle = (x - high).astype(BF16).astype(F32)
    return high, middle, x - high - middle


def loads_kernel(nc, lam_ref, table_ref, stiff_ref, mass_ref, dofs_ref, slab_ref, var_ref,
                 send_ref, slope_ref, mode_at, loads):
    ed, count = dofs_ref.shape
    lanes = table_ref.shape[1]
    cap = send_ref.shape[2]
    per_slab = table_ref.shape[0] // nc
    lam = lam_ref[0]
    dofs, slab, var = dofs_ref[...], slab_ref[...], var_ref[...]
    row_of = slab * per_slab + lax.shift_right_logical(dofs, 7)
    lane_of = jnp.bitwise_and(dofs, lanes - 1)
    chunks = count // lanes

    def look(step, found):
        found = list(found)
        for inner in range(8):
            r = step * 8 + inner
            row = jnp.broadcast_to(table_ref[pl.ds(r, 1), :], (ed, lanes))
            for c in range(chunks):
                at = slice(c * lanes, (c + 1) * lanes)
                taken = jnp.take_along_axis(row, lane_of[:, at], axis=1, mode="promise_in_bounds")
                found[c] = jnp.where(row_of[:, at] == r, taken, found[c])
        return tuple(found)

    found = lax.fori_loop(0, table_ref.shape[0] // 8, look, (jnp.zeros((ed, lanes), F32),) * chunks)
    for c in range(chunks):
        mode_at[:, c * lanes : (c + 1) * lanes] = found[c]
    modes = mode_at[...]
    for i in range(ed):
        operator = stiff_ref[i] - lam * mass_ref[i]
        loads[i : i + 1, :] = -jnp.sum(operator * modes, axis=0, keepdims=True)
    values = loads[...]
    quadratic = -jnp.sum(modes * values, axis=0, keepdims=True)
    padded = slope_ref.shape[1]
    matches = (lax.broadcasted_iota(jnp.int32, (padded, count), 0) == var).astype(F32).astype(BF16)
    terms = jnp.concatenate(list(three_way(quadratic)) + [jnp.zeros((5, count), F32)], axis=0).astype(BF16)
    nt = (((1,), (1,)), ((), ()))
    sums = lax.dot_general(terms, matches, nt, preferred_element_type=F32)
    slope_ref[...] = jnp.broadcast_to(jnp.sum(sums, axis=0, keepdims=True), slope_ref.shape)
    merged = jnp.zeros((ed, count), F32)
    for i in range(ed):
        merged = merged + jnp.where(dofs == dofs[i : i + 1, :], values[i : i + 1, :], 0.0)
    onehot = (lax.broadcasted_iota(jnp.int32, (nc, count), 0) == slab).astype(F32)
    earlier = lax.broadcasted_iota(jnp.int32, (count, count), 0) < lax.broadcasted_iota(jnp.int32, (count, count), 1)
    rank_all = jnp.dot(onehot.astype(BF16), earlier.astype(F32).astype(BF16), preferred_element_type=F32)
    rank = jnp.sum(onehot * rank_all, axis=0, keepdims=True).astype(jnp.int32)
    slot = slab * cap + rank
    high, middle, low = three_way(merged)
    coarse = lax.shift_right_logical(dofs, 4).astype(F32)
    fine = jnp.bitwise_and(dofs, 15).astype(F32)
    var_rows = jnp.concatenate([var.astype(F32), jnp.zeros((7, count), F32)], axis=0)
    data = jnp.concatenate([high, middle, low, coarse, fine, var_rows], axis=0).astype(BF16)
    for k in range(nc):
        place = (lax.broadcasted_iota(jnp.int32, (cap, count), 0) + k * cap == slot).astype(F32).astype(BF16)
        packed = lax.dot_general(data, place, nt, preferred_element_type=F32)
        send_ref[k, 0:ed, :] = (packed[0:ed] + packed[ed : 2 * ed]) + packed[2 * ed : 3 * ed]
        send_ref[k, ed : 2 * ed, :] = packed[3 * ed : 4 * ed] * 16.0 + packed[4 * ed : 5 * ed]
        send_ref[k, 2 * ed : 2 * ed + 8, :] = packed[5 * ed : 5 * ed + 8]


def solve_kernel(nc, nb, diag_ref, coup_ref, got_ref, slope_ref, mass_ref, out_ref, slope_out,
                 dbuf, cbuf, dsplit, csplit, spread_ref, rpart, rbuf, sl_chain, sl_band,
                 part, slots, piece, full, ybuf, xbuf,
                 mat, own_send, relay_send, slc_send, slc_recv, slb_send, slb_recv, r_send, r_recv,
                 rs_send, rs_recv, ag_send, ag_recv, out_send, out_recv):
    me, band = lax.axis_index("chain"), lax.axis_index("band")
    x_len = nc // 2
    my_x, core = me // 2, lax.rem(me, 2)
    rows, width = part.shape
    cols = width // nb
    nvars = rpart.shape[0]
    sibling = 2 * my_x + 1 - core
    blocks = (dbuf, cbuf)
    nt = (((1,), (1,)), ((), ()))
    nn = (((1,), (0,)), ((), ()))

    def at_band(b):
        return pl.ds(pl.multiple_of(b * cols, cols), cols)

    def at_group(c):
        return pl.ds(pl.multiple_of(c * rows, 8), rows)

    def along_x(by):
        return 2 * lax.rem(my_x + by + x_len, x_len) + core

    def remote(src, dst, send, recv, chain, to_band):
        return pltpu.make_async_remote_copy(src_ref=src, dst_ref=dst, send_sem=send, recv_sem=recv,
                                            device_id=(chain, to_band), device_id_type=MESH)

    def each_block(which, work):
        if which == 0:
            work()
        else:
            pl.when(me != 0)(work)

    def own_load(which):
        return pltpu.make_async_copy((diag_ref, coup_ref)[which], blocks[which].at[me], mat.at[which, me])

    def own_copy(which, i):
        to = (along_x(1), along_x(-1), sibling)[i]
        return remote((diag_ref, coup_ref)[which], blocks[which].at[me], own_send.at[which, i], mat.at[which, me], to, band)

    for which in range(2):
        each_block(which, lambda which=which: own_load(which).start())

    barrier = pltpu.get_barrier_semaphore()
    for r in range(1, nb):
        pl.semaphore_signal(barrier, inc=1, device_id=(me, lax.rem(band + r, nb)), device_id_type=MESH)
    for r in range(1, nc):
        pl.semaphore_signal(barrier, inc=1, device_id=(lax.rem(me + r, nc), band), device_id_type=MESH)
    pl.semaphore_wait(barrier, nb + nc - 2)

    def slope_chain_copy(to, source):
        return remote(slope_ref, sl_chain.at[source], slc_send.at[to], slc_recv.at[source], to, band)

    for r in range(1, nc):
        slope_chain_copy(lax.rem(me + r, nc), me).start()
    sl_chain[me] = slope_ref[...]

    def send_own(which):
        for i in range(3):
            own_copy(which, i).start()

    for which in range(2):
        each_block(which, functools.partial(send_own, which))

    def relay_copies(which, by):
        slab = along_x(-by)
        block = blocks[which].at[slab]
        on = remote(block, block, relay_send.at[which, by, 0], mat.at[which, slab], sibling, band)
        further = remote(block, block, relay_send.at[which, by, 1], mat.at[which, slab], along_x(1 if by == 1 else -1), band)
        return slab, on, further

    def forwards(by):
        return {1: core == 0, 3: core == 1}[by]

    def relay(which, by):
        slab, on, further = relay_copies(which, by)

        def work():
            pltpu.make_async_copy(blocks[which].at[slab], blocks[which].at[slab], mat.at[which, slab]).wait()
            on.start()
            if by != 2:
                pl.when(forwards(by))(lambda: further.start())

        if which == 0:
            work()
        else:
            pl.when(slab != 0)(work)

    def relay_farthest(which, k):
        pl.when(k == along_x(2))(lambda: relay(which, 2))

    cap = got_ref.shape[2]
    ed = (got_ref.shape[1] - 8) // 2
    block = spread_ref.shape[0]
    lines = 128
    base = lax.broadcasted_iota(jnp.int32, (lines, cap), 0)
    variable = lax.broadcasted_iota(jnp.int32, (nvars, cap), 0)
    matches = [(variable == got_ref[s, 2 * ed : 2 * ed + 1, :].astype(jnp.int32)).astype(F32).astype(BF16) for s in range(nc)]
    matches = jnp.concatenate(matches + matches, axis=1)

    def one_block(n, carry):
        def one_source(s, inner):
            values = got_ref[s, 0:ed, :]
            dofs = got_ref[s, ed : 2 * ed, :].astype(jnp.int32) - n * block
            for half in range(block // lines):
                total = jnp.zeros((lines, cap), F32)
                for i in range(ed):
                    hit = base == dofs[i : i + 1, :] - half * lines
                    total = jnp.where(hit, values[i : i + 1, :], total)
                high = total.astype(BF16)
                at = pl.ds(pl.multiple_of(s * cap, cap), cap)
                spread_ref[half * lines : (half + 1) * lines, at] = high
                at = pl.ds(pl.multiple_of((s + nc) * cap, cap), cap)
                spread_ref[half * lines : (half + 1) * lines, at] = (total - high.astype(F32)).astype(BF16)
            return inner

        lax.fori_loop(0, nc, one_source, 0)
        at = pl.ds(pl.multiple_of(n * block, block), block)
        rpart[:, at] = lax.dot_general(matches, spread_ref[...], nt, preferred_element_type=F32)
        return carry

    lax.fori_loop(0, width // block, one_block, 0)

    for r in range(1, nc):
        slope_chain_copy(me, lax.rem(me + r, nc)).wait_recv()
    total = sl_chain[0]
    for c in range(1, nc):
        total = total + sl_chain[c]

    def slope_band_copy(r):
        to = lax.rem(band + r, nb)
        return remote(sl_band.at[band], sl_band.at[band], slb_send.at[r], slb_recv.at[r], me, to)

    def slope_band_arrival(r):
        source = lax.rem(band - r + nb, nb)
        return remote(sl_band.at[source], sl_band.at[source], slb_send.at[r], slb_recv.at[r], me, source)

    sl_band[band] = total
    for r in range(1, nb):
        slope_band_copy(r).start()
    for by in (1, 3):
        relay(0, by)
    for r in range(1, nb):
        slope_band_arrival(r).wait_recv()
    total = sl_band[0]
    for b in range(1, nb):
        total = total + sl_band[b]
    slope_out[...] = total[0:1, :nvars]
    line = lax.broadcasted_iota(jnp.int32, total.shape, 0)
    high, middle, low = three_way(total)
    slope_terms = jnp.where((line == 0) | (line == 3) | (line == 5), high, 0.0)
    slope_terms = jnp.where((line == 1) | (line == 4), middle, jnp.where(line == 2, low, slope_terms))
    line = lax.broadcasted_iota(jnp.int32, (8, cols), 0)
    high, middle, low = three_way(jnp.broadcast_to(mass_ref[...], (8, cols)))
    mass_terms = jnp.where(line < 3, high, jnp.where(line < 5, middle, jnp.where(line == 5, low, 0.0)))
    outer = lax.dot_general(slope_terms.astype(BF16), mass_terms.astype(BF16), (((0,), (0,)), ((), ())), preferred_element_type=F32)
    rpart[:, at_band(band)] = rpart[:, at_band(band)] + outer[:nvars]

    def rhs_copy(to, source):
        return remote(rpart.at[at_group(to), :], rbuf.at[source], r_send.at[to], r_recv.at[source], to, band)

    for r in range(1, nc):
        rhs_copy(lax.rem(me + r, nc), me).start()
    rbuf[me] = rpart[at_group(me), :]
    for by in (1, 3):
        relay(1, by)

    def rhs_wait(k):
        pl.when(k != me)(lambda: rhs_copy(me, k).wait_recv())

    def rs_copy(r):
        to = lax.rem(band + r, nb)
        return remote(part.at[:, at_band(to)], slots.at[r], rs_send.at[r], rs_recv.at[r], me, to)

    def ag_copy(r):
        to = lax.rem(band + r, nb)
        return remote(piece, full.at[:, at_band(band)], ag_send.at[r], ag_recv.at[r], me, to)

    def ag_arrival(r):
        source = lax.rem(band - r + nb, nb)
        return remote(piece, full.at[:, at_band(source)], ag_send.at[r], ag_recv.at[r], me, source)

    def reduce_start():
        for r in range(1, nb):
            rs_copy(r).start()

    def reduce_end():
        total = part[:, at_band(band)]
        for r in range(1, nb):
            rs_copy(r).wait_recv()
            total = total + slots[r]
        for r in range(1, nb):
            rs_copy(r).wait_send()
        return total

    def gather_start(value):
        piece[...] = value
        for r in range(1, nb):
            ag_copy(r).start()
        full[:, at_band(band)] = value

    def gather_end():
        for r in range(1, nb):
            ag_arrival(r).wait_recv()
        for r in range(1, nb):
            ag_copy(r).wait_send()

    def block_wait(which, k):
        @pl.when((lax.rem(k, 2) != core) | (k == me))
        def _():
            pltpu.make_async_copy(blocks[which].at[k], blocks[which].at[k], mat.at[which, k]).wait()

    def split_diag(k):
        block_wait(0, k)
        high, low = split2(dbuf[k])
        dsplit[k, 0:cols, :] = high
        dsplit[k, cols : 2 * cols, :] = low

    def split_coup(k):
        block_wait(1, k)
        high, low = split2(cbuf[k])
        csplit[k, :, 0:cols] = high
        csplit[k, :, cols : 2 * cols] = low

    def narrow(value, weights, dims):
        wide = lax.dot_general(stacked_rows(value), weights, dims, preferred_element_type=F32)
        return (wide[:rows, :cols] + wide[:rows, cols:]) + (wide[rows:, :cols] + wide[rows:, cols:])

    def spread(value, weights, dims):
        both = stacked_rows(value)
        both = jnp.concatenate([both, both], axis=1)
        wide = lax.dot_general(both, weights, dims, preferred_element_type=F32)
        return wide[:rows] + wide[rows:]

    rhs_wait(0)
    part[...] = rbuf[0]
    relay_farthest(0, 0)

    def forward(k, carry):
        reduce_start()
        relay_farthest(0, k + 1)
        relay_farthest(1, k + 1)
        split_diag(k)
        gather_start(reduce_end())

        @pl.when(k + 1 < nc)
        def _():
            split_coup(k + 1)

        gather_end()
        solved = narrow(full[...], dsplit[k], nt)
        ybuf[k] = solved

        @pl.when(k + 1 < nc)
        def _():
            rhs_wait(k + 1)
            part[...] = rbuf[k + 1] - spread(solved, csplit[k + 1], nt)

        return carry

    lax.fori_loop(0, nc, forward, 0)

    def out_copy(k, source):
        return remote(xbuf.at[k], out_ref.at[at_group(source), :], out_send.at[k], out_recv.at[source], k, band)

    def backward(step, coupled):
        k = nc - 1 - step
        part[...] = spread(ybuf[k] - coupled, dsplit[k], nn)
        reduce_start()
        total = reduce_end()
        gather_start(total)
        xbuf[k] = total

        @pl.when(k != me)
        def _():
            out_copy(k, me).start()

        @pl.when(k == me)
        def _():
            out_ref[at_group(me), :] = total

        gather_end()
        return narrow(full[...], csplit[k], nn)

    coupled = lax.fori_loop(0, nc - 1, backward, jnp.zeros((rows, cols), F32))
    part[...] = spread(ybuf[0] - coupled, dsplit[0], nn)
    reduce_start()
    total = reduce_end()
    xbuf[0] = total
    pl.when(me != 0)(lambda: out_copy(0, me).start())

    @pl.when(me == 0)
    def _():
        out_ref[at_group(0), :] = total

    for r in range(1, nc):
        other = lax.rem(me + r, nc)
        out_copy(other, me).wait_send()
        out_copy(me, other).wait_recv()
        rhs_copy(other, me).wait_send()
        slope_chain_copy(other, me).wait_send()
    for r in range(1, nb):
        slope_band_copy(r).wait_send()

    def sent(which):
        for i in range(3):
            own_copy(which, i).wait_send()

    for which in range(2):
        each_block(which, functools.partial(sent, which))
        for by in (1, 2, 3):
            slab, on, further = relay_copies(which, by)

            def relayed(on=on, further=further, by=by):
                on.wait_send()
                if by != 2:
                    pl.when(forwards(by))(lambda: further.wait_send())

            if which == 0:
                relayed()
            else:
                pl.when(slab != 0)(relayed)


def on_device(nc, nb, diag_inverse, coupling, elem_stiff, elem_mass, elem_dofs, elem_slab, elem_var, mode, mass_mode, eigenvalue):
    band = lax.axis_index("band")
    cols, width = diag_inverse.shape
    ed, count = elem_dofs.shape
    cap = count // 4
    rows = VARS // nc
    everyone = nc * nb
    padded = 256
    vmem = pl.BlockSpec(memory_space=pltpu.VMEM)
    anywhere = pl.BlockSpec(memory_space=pl.ANY)
    table = lax.all_to_all(jnp.broadcast_to(mode[None, :], (everyone, cols)), ("chain", "band"), 0, 0, tiled=True)
    send, slope = pl.pallas_call(
        functools.partial(loads_kernel, nc),
        out_shape=(jax.ShapeDtypeStruct((nc, 2 * ed + 8, cap), F32), jax.ShapeDtypeStruct((8, padded), F32)),
        in_specs=[pl.BlockSpec(memory_space=pltpu.SMEM)] + [vmem] * 6,
        out_specs=(vmem, vmem),
        scratch_shapes=[pltpu.VMEM((ed, count), F32), pltpu.VMEM((ed, count), F32)],
        compiler_params=pltpu.CompilerParams(vmem_limit_bytes=30 * 1024 * 1024),
        cost_estimate=pl.CostEstimate(flops=2 * 10**9, bytes_accessed=10**7, transcendentals=0),
        name="loads",
    )(eigenvalue, table, elem_stiff, elem_mass, elem_dofs, elem_slab.reshape(1, count), elem_var.reshape(1, count))
    got = lax.all_to_all(send, "chain", 0, 0, tiled=True)
    own_mass = lax.dynamic_slice_in_dim(mass_mode, band * cols, cols)[None, :]
    dma = pltpu.SemaphoreType.DMA
    eigvec_slope, eigval_slope = pl.pallas_call(
        functools.partial(solve_kernel, nc, nb),
        out_shape=(jax.ShapeDtypeStruct((VARS, cols), F32), jax.ShapeDtypeStruct((1, VARS), F32)),
        in_specs=[anywhere, anywhere, vmem, vmem, vmem],
        out_specs=(vmem, vmem),
        scratch_shapes=[
            pltpu.VMEM((nc, cols, width), F32),
            pltpu.VMEM((nc, width, cols), F32),
            pltpu.VMEM((nc, 2 * cols, width), BF16),
            pltpu.VMEM((nc, width, 2 * cols), BF16),
            pltpu.VMEM((256, 2 * nc * cap), BF16),
            pltpu.VMEM((VARS, width), F32),
            pltpu.VMEM((nc, rows, width), F32),
            pltpu.VMEM((nc, 8, padded), F32),
            pltpu.VMEM((nb, 8, padded), F32),
            pltpu.VMEM((rows, width), F32),
            pltpu.VMEM((nb, rows, cols), F32),
            pltpu.VMEM((rows, cols), F32),
            pltpu.VMEM((rows, width), F32),
            pltpu.VMEM((nc, rows, cols), F32),
            pltpu.VMEM((nc, rows, cols), F32),
            dma((2, nc)), dma((2, 3)), dma((2, 4, 2)),
            dma((nc,)), dma((nc,)), dma((nb,)), dma((nb,)), dma((nc,)), dma((nc,)),
            dma((nb,)), dma((nb,)), dma((nb,)), dma((nb,)), dma((nc,)), dma((nc,)),
        ],
        compiler_params=pltpu.CompilerParams(collective_id=0, has_side_effects=True, vmem_limit_bytes=52 * 1024 * 1024),
        cost_estimate=pl.CostEstimate(flops=10**10, bytes_accessed=10**8, transcendentals=0),
        name="solve",
    )(diag_inverse, coupling, got, slope, own_mass)
    return eigvec_slope, eigval_slope.reshape(VARS)


def solution(mesh):
    nc, nb = mesh.shape["chain"], mesh.shape["band"]
    in_specs = (
        P(("chain", "band"), None),
        P("chain", "band"),
        P(None, None, ("chain", "band")),
        P(None, None, ("chain", "band")),
        P(None, ("chain", "band")),
        P(("chain", "band"), None),
        P(("chain", "band")),
        P(("chain", "band")),
        P("chain"),
        P(),
    )
    out_specs = (P(None, ("chain", "band")), P())
    return jax.shard_map(functools.partial(on_device, nc, nb), mesh=mesh, in_specs=in_specs, out_specs=out_specs, check_vma=False)
```

```python
import functools

import jax
import jax.numpy as jnp
from jax import lax
from jax.experimental import pallas as pl
from jax.experimental.pallas import tpu as pltpu
from jax.sharding import PartitionSpec as P

MESH = pl.DeviceIdType.MESH
F32 = jnp.float32
BF16 = jnp.bfloat16
VARS = 192


def split2(x):
    high = x.astype(BF16)
    return high, (x - high.astype(F32)).astype(BF16)


def stacked_rows(x):
    high = x.astype(BF16).astype(F32)
    return jnp.concatenate([high, x - high], axis=0).astype(BF16)


def three_way(x):
    high = x.astype(BF16).astype(F32)
    middle = (x - high).astype(BF16).astype(F32)
    return high, middle, x - high - middle


def element_loads(nc, lam_ref, table_ref, stiff_ref, mass_ref, dofs_ref, slab_ref, var_ref,
                  send_ref, slope_ref, mode_at, loads, matrices_here):
    ed, count = dofs_ref.shape
    lanes = table_ref.shape[1]
    cap = send_ref.shape[2]
    lam = lam_ref[0]
    dofs, slab, var = dofs_ref[...], slab_ref[...], var_ref[...]
    row_of = lax.shift_right_logical(dofs, 7) * nc + slab
    lane_of = jnp.bitwise_and(dofs, lanes - 1)
    chunks = count // lanes

    def look(step, found):
        found = list(found)
        for inner in range(8):
            r = step * 8 + inner
            row = jnp.broadcast_to(table_ref[pl.ds(r, 1), :], (ed, lanes))
            for c in range(chunks):
                at = slice(c * lanes, (c + 1) * lanes)
                taken = jnp.take_along_axis(row, lane_of[:, at], axis=1, mode="promise_in_bounds")
                found[c] = jnp.where(row_of[:, at] == r, taken, found[c])
        return tuple(found)

    found = lax.fori_loop(0, table_ref.shape[0] // 8, look, (jnp.zeros((ed, lanes), F32),) * chunks)
    for c in range(chunks):
        mode_at[:, c * lanes : (c + 1) * lanes] = found[c]
    modes = mode_at[...]
    matrices_here()
    for i in range(ed):
        operator = stiff_ref[i] - lam * mass_ref[i]
        loads[i : i + 1, :] = -jnp.sum(operator * modes, axis=0, keepdims=True)
    values = loads[...]
    quadratic = -jnp.sum(modes * values, axis=0, keepdims=True)
    padded = slope_ref.shape[1]
    matches = (lax.broadcasted_iota(jnp.int32, (padded, count), 0) == var).astype(F32).astype(BF16)
    terms = jnp.concatenate(list(three_way(quadratic)) + [jnp.zeros((5, count), F32)], axis=0).astype(BF16)
    nt = (((1,), (1,)), ((), ()))
    sums = lax.dot_general(terms, matches, nt, preferred_element_type=F32)
    slope_ref[...] = jnp.broadcast_to(jnp.sum(sums, axis=0, keepdims=True), slope_ref.shape)
    merged = jnp.zeros((ed, count), F32)
    for i in range(ed):
        merged = merged + jnp.where(dofs == dofs[i : i + 1, :], values[i : i + 1, :], 0.0)
    onehot = (lax.broadcasted_iota(jnp.int32, (nc, count), 0) == slab).astype(F32)
    earlier = lax.broadcasted_iota(jnp.int32, (count, count), 0) < lax.broadcasted_iota(jnp.int32, (count, count), 1)
    rank_all = jnp.dot(onehot.astype(BF16), earlier.astype(F32).astype(BF16), preferred_element_type=F32)
    rank = jnp.sum(onehot * rank_all, axis=0, keepdims=True).astype(jnp.int32)
    slot = slab * cap + rank
    high, middle, low = three_way(merged)
    coarse = lax.shift_right_logical(dofs, 4).astype(F32)
    fine = jnp.bitwise_and(dofs, 15).astype(F32)
    var_rows = jnp.concatenate([var.astype(F32), jnp.zeros((7, count), F32)], axis=0)
    data = jnp.concatenate([high, middle, low, coarse, fine, var_rows], axis=0).astype(BF16)
    for k in range(nc):
        place = (lax.broadcasted_iota(jnp.int32, (cap, count), 0) + k * cap == slot).astype(F32).astype(BF16)
        packed = lax.dot_general(data, place, nt, preferred_element_type=F32)
        send_ref[k, 0:ed, :] = (packed[0:ed] + packed[ed : 2 * ed]) + packed[2 * ed : 3 * ed]
        send_ref[k, ed : 2 * ed, :] = packed[3 * ed : 4 * ed] * 16.0 + packed[4 * ed : 5 * ed]
        send_ref[k, 2 * ed : 2 * ed + 8, :] = packed[5 * ed : 5 * ed + 8]


def solve_kernel(nc, nb, lam_ref, diag_ref, coup_ref, stiff_ref, emass_ref, dofs_ref, slab_ref, var_ref, mode_ref, mass_ref,
                 out_ref, slope_out, stiff, emass, mode_tile, mode_chain, mode_group, table, mode_at, loads, send_ref, got_ref, slope_ref,
                 dbuf, cbuf, dsplit, csplit, spread_ref, rpart, rbuf, sl_chain, sl_band,
                 part, slots, piece, full, ybuf, xbuf,
                 el_sem, mc_send, mc_recv, mb_send, mb_recv, ex_send, ex_recv, mat, own_send, relay_send, slc_send, slc_recv, slb_send, slb_recv, r_send, r_recv,
                 rs_send, rs_recv, ag_send, ag_recv, out_send, out_recv):
    me, band = lax.axis_index("chain"), lax.axis_index("band")
    x_len = nc // 2
    my_x, core = me // 2, lax.rem(me, 2)
    rows, width = part.shape
    cols = width // nb
    nvars = rpart.shape[0]
    sibling = 2 * my_x + 1 - core
    blocks = (dbuf, cbuf)
    nt = (((1,), (1,)), ((), ()))
    nn = (((1,), (0,)), ((), ()))

    def at_band(b):
        return pl.ds(pl.multiple_of(b * cols, cols), cols)

    def at_group(c):
        return pl.ds(pl.multiple_of(c * rows, 8), rows)

    def along_x(by):
        return 2 * lax.rem(my_x + by + x_len, x_len) + core

    def remote(src, dst, send, recv, chain, to_band):
        return pltpu.make_async_remote_copy(src_ref=src, dst_ref=dst, send_sem=send, recv_sem=recv,
                                            device_id=(chain, to_band), device_id_type=MESH)

    def each_block(which, work):
        if which == 0:
            work()
        else:
            pl.when(me != 0)(work)

    def own_load(which):
        return pltpu.make_async_copy((diag_ref, coup_ref)[which], blocks[which].at[me], mat.at[which, me])

    def own_copy(which, i):
        to = (along_x(1), along_x(-1), sibling)[i]
        return remote((diag_ref, coup_ref)[which], blocks[which].at[me], own_send.at[which, i], mat.at[which, me], to, band)

    stiff_load = pltpu.make_async_copy(stiff_ref, stiff, el_sem.at[0])
    emass_load = pltpu.make_async_copy(emass_ref, emass, el_sem.at[1])
    stiff_load.start()
    emass_load.start()
    for which in range(2):
        each_block(which, lambda which=which: own_load(which).start())
    mode_tile[...] = jnp.broadcast_to(mode_ref[...], mode_tile.shape)

    barrier = pltpu.get_barrier_semaphore()
    for r in range(1, nb):
        pl.semaphore_signal(barrier, inc=1, device_id=(me, lax.rem(band + r, nb)), device_id_type=MESH)
    for r in range(1, nc):
        pl.semaphore_signal(barrier, inc=1, device_id=(lax.rem(me + r, nc), band), device_id_type=MESH)
    pl.semaphore_wait(barrier, nb + nc - 2)

    def mode_chain_copy(to, source):
        return remote(mode_tile, mode_chain.at[source], mc_send.at[to], mc_recv.at[source], to, band)

    for r in range(1, nc):
        mode_chain_copy(lax.rem(me + r, nc), me).start()
    mode_chain[me] = mode_tile[...]

    def send_own(which):
        for i in range(3):
            own_copy(which, i).start()

    pl.when(core == 0)(lambda: send_own(0))
    for r in range(1, nc):
        mode_chain_copy(me, lax.rem(me + r, nc)).wait_recv()
    line = lax.broadcasted_iota(jnp.int32, (nc, cols), 0)
    whole = jnp.zeros((nc, cols), F32)
    for c in range(nc):
        whole = jnp.where(line == c, mode_chain[c], whole)
    mode_group[...] = whole

    def at_rows(b):
        return table.at[pl.ds(pl.multiple_of(b * nc, 8), nc), :]

    def mode_band_copy(r):
        to = lax.rem(band + r, nb)
        return remote(mode_group, at_rows(band), mb_send.at[r], mb_recv.at[r], me, to)

    def mode_band_arrival(r):
        source = lax.rem(band - r + nb, nb)
        return remote(mode_group, at_rows(source), mb_send.at[r], mb_recv.at[r], me, source)

    for r in range(1, nb):
        mode_band_copy(r).start()
    table[pl.ds(pl.multiple_of(band * nc, 8), nc), :] = whole
    for r in range(1, nb):
        mode_band_arrival(r).wait_recv()

    def matrices_here():
        stiff_load.wait()
        emass_load.wait()

    element_loads(nc, lam_ref, table, stiff, emass, dofs_ref, slab_ref, var_ref, send_ref, slope_ref, mode_at, loads, matrices_here)

    def element_copy(to, source):
        return remote(send_ref.at[to], got_ref.at[source], ex_send.at[to], ex_recv.at[source], to, band)

    def slope_chain_copy(to, source):
        return remote(slope_ref, sl_chain.at[source], slc_send.at[to], slc_recv.at[source], to, band)

    for r in range(1, nc):
        element_copy(lax.rem(me + r, nc), me).start()
        slope_chain_copy(lax.rem(me + r, nc), me).start()
    sl_chain[me] = slope_ref[...]
    got_ref[me] = send_ref[me]
    pl.when(core == 1)(lambda: send_own(0))
    each_block(1, lambda: send_own(1))
    for r in range(1, nc):
        element_copy(me, lax.rem(me + r, nc)).wait_recv()

    def relay_on(which, by):
        slab = along_x(-by)
        block = blocks[which].at[slab]
        return remote(block, block, relay_send.at[which, by, 0], mat.at[which, slab], sibling, band)

    def relay_further(which, by):
        slab = along_x(-by)
        block = blocks[which].at[slab]
        return remote(block, block, relay_send.at[which, by, 1], mat.at[which, slab], along_x(1 if by == 1 else -1), band)

    def each_relayed(which, by, work):
        if which == 0:
            work()
        else:
            pl.when(along_x(-by) != 0)(work)

    def forwards(by):
        return {1: core == 0, 3: core == 1}[by]

    def relay(which, by):
        slab = along_x(-by)

        def work():
            pltpu.make_async_copy(blocks[which].at[slab], blocks[which].at[slab], mat.at[which, slab]).wait()
            if by != 2:
                pl.when(forwards(by))(lambda: relay_further(which, by).start())
            relay_on(which, by).start()

        each_relayed(which, by, work)

    def relay_farthest(which, k):
        pl.when(k == along_x(2))(lambda: relay(which, 2))

    cap = got_ref.shape[2]
    ed = (got_ref.shape[1] - 8) // 2
    block = spread_ref.shape[0]
    lines = 128
    base = lax.broadcasted_iota(jnp.int32, (lines, cap), 0)
    variable = lax.broadcasted_iota(jnp.int32, (nvars, cap), 0)
    matches = [(variable == got_ref[s, 2 * ed : 2 * ed + 1, :].astype(jnp.int32)).astype(F32).astype(BF16) for s in range(nc)]
    matches = jnp.concatenate(matches + matches, axis=1)

    def one_block(n, carry):
        def one_source(s, inner):
            values = got_ref[s, 0:ed, :]
            dofs = got_ref[s, ed : 2 * ed, :].astype(jnp.int32) - n * block
            for half in range(block // lines):
                total = jnp.zeros((lines, cap), F32)
                for i in range(ed):
                    hit = base == dofs[i : i + 1, :] - half * lines
                    total = jnp.where(hit, values[i : i + 1, :], total)
                high = total.astype(BF16)
                at = pl.ds(pl.multiple_of(s * cap, cap), cap)
                spread_ref[half * lines : (half + 1) * lines, at] = high
                at = pl.ds(pl.multiple_of((s + nc) * cap, cap), cap)
                spread_ref[half * lines : (half + 1) * lines, at] = (total - high.astype(F32)).astype(BF16)
            return inner

        lax.fori_loop(0, nc, one_source, 0)
        at = pl.ds(pl.multiple_of(n * block, block), block)
        rpart[:, at] = lax.dot_general(matches, spread_ref[...], nt, preferred_element_type=F32)
        return carry

    lax.fori_loop(0, width // block, one_block, 0)

    for r in range(1, nc):
        slope_chain_copy(me, lax.rem(me + r, nc)).wait_recv()
    total = sl_chain[0]
    for c in range(1, nc):
        total = total + sl_chain[c]

    def slope_band_copy(r):
        to = lax.rem(band + r, nb)
        return remote(sl_band.at[band], sl_band.at[band], slb_send.at[r], slb_recv.at[r], me, to)

    def slope_band_arrival(r):
        source = lax.rem(band - r + nb, nb)
        return remote(sl_band.at[source], sl_band.at[source], slb_send.at[r], slb_recv.at[r], me, source)

    sl_band[band] = total
    for r in range(1, nb):
        slope_band_copy(r).start()
    for by in (1, 3):
        relay(0, by)
    for r in range(1, nb):
        slope_band_arrival(r).wait_recv()
    total = sl_band[0]
    for b in range(1, nb):
        total = total + sl_band[b]
    slope_out[...] = total[0:1, :nvars]
    line = lax.broadcasted_iota(jnp.int32, total.shape, 0)
    high, middle, low = three_way(total)
    slope_terms = jnp.where((line == 0) | (line == 3) | (line == 5), high, 0.0)
    slope_terms = jnp.where((line == 1) | (line == 4), middle, jnp.where(line == 2, low, slope_terms))
    line = lax.broadcasted_iota(jnp.int32, (8, cols), 0)
    high, middle, low = three_way(jnp.broadcast_to(mass_ref[...], (8, cols)))
    mass_terms = jnp.where(line < 3, high, jnp.where(line < 5, middle, jnp.where(line == 5, low, 0.0)))
    outer = lax.dot_general(slope_terms.astype(BF16), mass_terms.astype(BF16), (((0,), (0,)), ((), ())), preferred_element_type=F32)
    rpart[:, at_band(band)] = rpart[:, at_band(band)] + outer[:nvars]

    def rhs_copy(to, source):
        return remote(rpart.at[at_group(to), :], rbuf.at[source], r_send.at[to], r_recv.at[source], to, band)

    for r in range(1, nc):
        rhs_copy(lax.rem(me + r, nc), me).start()
    rbuf[me] = rpart[at_group(me), :]
    for by in (1, 3):
        relay(1, by)

    def rhs_wait(k):
        pl.when(k != me)(lambda: rhs_copy(me, k).wait_recv())

    def rs_copy(r):
        to = lax.rem(band + r, nb)
        return remote(part.at[:, at_band(to)], slots.at[r], rs_send.at[r], rs_recv.at[r], me, to)

    def ag_copy(r):
        to = lax.rem(band + r, nb)
        return remote(piece, full.at[:, at_band(band)], ag_send.at[r], ag_recv.at[r], me, to)

    def ag_arrival(r):
        source = lax.rem(band - r + nb, nb)
        return remote(piece, full.at[:, at_band(source)], ag_send.at[r], ag_recv.at[r], me, source)

    def reduce_start():
        for r in range(1, nb):
            rs_copy(r).start()

    def reduce_end():
        total = part[:, at_band(band)]
        for r in range(1, nb):
            rs_copy(r).wait_recv()
            total = total + slots[r]
        for r in range(1, nb):
            rs_copy(r).wait_send()
        return total

    def gather_start(value):
        piece[...] = value
        for r in range(1, nb):
            ag_copy(r).start()
        full[:, at_band(band)] = value

    def gather_end():
        for r in range(1, nb):
            ag_arrival(r).wait_recv()
        for r in range(1, nb):
            ag_copy(r).wait_send()

    def block_wait(which, k):
        @pl.when((lax.rem(k, 2) != core) | (k == me))
        def _():
            pltpu.make_async_copy(blocks[which].at[k], blocks[which].at[k], mat.at[which, k]).wait()

    def split_diag(k):
        block_wait(0, k)
        high, low = split2(dbuf[k])
        dsplit[k, 0:cols, :] = high
        dsplit[k, cols : 2 * cols, :] = low

    def split_coup(k):
        block_wait(1, k)
        high, low = split2(cbuf[k])
        csplit[k, :, 0:cols] = high
        csplit[k, :, cols : 2 * cols] = low

    def narrow(value, weights, dims):
        wide = lax.dot_general(stacked_rows(value), weights, dims, preferred_element_type=F32)
        return (wide[:rows, :cols] + wide[:rows, cols:]) + (wide[rows:, :cols] + wide[rows:, cols:])

    def spread(value, weights, dims):
        both = stacked_rows(value)
        both = jnp.concatenate([both, both], axis=1)
        wide = lax.dot_general(both, weights, dims, preferred_element_type=F32)
        return wide[:rows] + wide[rows:]

    rhs_wait(0)
    part[...] = rbuf[0]
    relay_farthest(0, 0)

    def forward(k, carry):
        reduce_start()
        relay_farthest(0, k + 1)
        relay_farthest(1, k + 1)
        split_diag(k)
        gather_start(reduce_end())

        @pl.when(k + 1 < nc)
        def _():
            split_coup(k + 1)

        gather_end()
        solved = narrow(full[...], dsplit[k], nt)
        ybuf[k] = solved

        @pl.when(k + 1 < nc)
        def _():
            rhs_wait(k + 1)
            part[...] = rbuf[k + 1] - spread(solved, csplit[k + 1], nt)

        return carry

    lax.fori_loop(0, nc, forward, 0)

    def out_copy(k, source):
        return remote(xbuf.at[k], out_ref.at[at_group(source), :], out_send.at[k], out_recv.at[source], k, band)

    def backward(step, coupled):
        k = nc - 1 - step
        part[...] = spread(ybuf[k] - coupled, dsplit[k], nn)
        reduce_start()
        total = reduce_end()
        gather_start(total)
        xbuf[k] = total

        @pl.when(k != me)
        def _():
            out_copy(k, me).start()

        @pl.when(k == me)
        def _():
            out_ref[at_group(me), :] = total

        gather_end()
        return narrow(full[...], csplit[k], nn)

    coupled = lax.fori_loop(0, nc - 1, backward, jnp.zeros((rows, cols), F32))
    part[...] = spread(ybuf[0] - coupled, dsplit[0], nn)
    reduce_start()
    total = reduce_end()
    xbuf[0] = total
    pl.when(me != 0)(lambda: out_copy(0, me).start())

    @pl.when(me == 0)
    def _():
        out_ref[at_group(0), :] = total

    for r in range(1, nc):
        other = lax.rem(me + r, nc)
        out_copy(other, me).wait_send()
        out_copy(me, other).wait_recv()
        rhs_copy(other, me).wait_send()
        slope_chain_copy(other, me).wait_send()
        mode_chain_copy(other, me).wait_send()
        element_copy(other, me).wait_send()
    for r in range(1, nb):
        slope_band_copy(r).wait_send()
        mode_band_copy(r).wait_send()

    def sent(which):
        for i in range(3):
            own_copy(which, i).wait_send()

    for which in range(2):
        each_block(which, functools.partial(sent, which))
        for by in (1, 2, 3):

            def relayed(which=which, by=by):
                relay_on(which, by).wait_send()
                if by != 2:
                    pl.when(forwards(by))(lambda: relay_further(which, by).wait_send())

            each_relayed(which, by, relayed)


def on_device(nc, nb, diag_inverse, coupling, elem_stiff, elem_mass, elem_dofs, elem_slab, elem_var, mode, mass_mode, eigenvalue):
    band = lax.axis_index("band")
    cols, width = diag_inverse.shape
    ed, count = elem_dofs.shape
    cap = count // 4
    rows = VARS // nc
    padded = 256
    vmem = pl.BlockSpec(memory_space=pltpu.VMEM)
    anywhere = pl.BlockSpec(memory_space=pl.ANY)
    own_mass = lax.dynamic_slice_in_dim(mass_mode, band * cols, cols)[None, :]
    dma = pltpu.SemaphoreType.DMA
    eigvec_slope, eigval_slope = pl.pallas_call(
        functools.partial(solve_kernel, nc, nb),
        out_shape=(jax.ShapeDtypeStruct((VARS, cols), F32), jax.ShapeDtypeStruct((1, VARS), F32)),
        in_specs=[pl.BlockSpec(memory_space=pltpu.SMEM)] + [anywhere] * 4 + [vmem] * 5,
        out_specs=(vmem, vmem),
        scratch_shapes=[
            pltpu.VMEM((ed, ed, count), F32),
            pltpu.VMEM((ed, ed, count), F32),
            pltpu.VMEM((8, cols), F32),
            pltpu.VMEM((nc, 8, cols), F32),
            pltpu.VMEM((nc, cols), F32),
            pltpu.VMEM((nc * nb, cols), F32),
            pltpu.VMEM((ed, count), F32),
            pltpu.VMEM((ed, count), F32),
            pltpu.VMEM((nc, 2 * ed + 8, cap), F32),
            pltpu.VMEM((nc, 2 * ed + 8, cap), F32),
            pltpu.VMEM((8, padded), F32),
            pltpu.VMEM((nc, cols, width), F32),
            pltpu.VMEM((nc, width, cols), F32),
            pltpu.VMEM((nc, 2 * cols, width), BF16),
            pltpu.VMEM((nc, width, 2 * cols), BF16),
            pltpu.VMEM((256, 2 * nc * cap), BF16),
            pltpu.VMEM((VARS, width), F32),
            pltpu.VMEM((nc, rows, width), F32),
            pltpu.VMEM((nc, 8, padded), F32),
            pltpu.VMEM((nb, 8, padded), F32),
            pltpu.VMEM((rows, width), F32),
            pltpu.VMEM((nb, rows, cols), F32),
            pltpu.VMEM((rows, cols), F32),
            pltpu.VMEM((rows, width), F32),
            pltpu.VMEM((nc, rows, cols), F32),
            pltpu.VMEM((nc, rows, cols), F32),
            dma((2,)), dma((nc,)), dma((nc,)), dma((nb,)), dma((nb,)), dma((nc,)), dma((nc,)),
            dma((2, nc)), dma((2, 3)), dma((2, 4, 2)),
            dma((nc,)), dma((nc,)), dma((nb,)), dma((nb,)), dma((nc,)), dma((nc,)),
            dma((nb,)), dma((nb,)), dma((nb,)), dma((nb,)), dma((nc,)), dma((nc,)),
        ],
        compiler_params=pltpu.CompilerParams(collective_id=0, has_side_effects=True, vmem_limit_bytes=52 * 1024 * 1024),
        cost_estimate=pl.CostEstimate(flops=10**10, bytes_accessed=10**8, transcendentals=0),
        name="solve",
    )(eigenvalue, diag_inverse, coupling, elem_stiff, elem_mass, elem_dofs, elem_slab.reshape(1, count),
      elem_var.reshape(1, count), mode[None, :], own_mass)
    return eigvec_slope, eigval_slope.reshape(VARS)


def solution(mesh):
    nc, nb = mesh.shape["chain"], mesh.shape["band"]
    in_specs = (
        P(("chain", "band"), None),
        P("chain", "band"),
        P(None, None, ("chain", "band")),
        P(None, None, ("chain", "band")),
        P(None, ("chain", "band")),
        P(("chain", "band"), None),
        P(("chain", "band")),
        P(("chain", "band")),
        P("chain"),
        P(),
    )
    out_specs = (P(None, ("chain", "band")), P())
    return jax.shard_map(functools.partial(on_device, nc, nb), mesh=mesh, in_specs=in_specs, out_specs=out_specs, check_vma=False)
```

```python
import functools
import math

import jax
import jax.numpy as jnp
from jax import lax
from jax.experimental import pallas as pl
from jax.experimental.pallas import tpu as pltpu
from jax.sharding import PartitionSpec as P

MESH = pl.DeviceIdType.MESH
F32 = jnp.float32
BF16 = jnp.bfloat16
VARS = 192


def split2(x):
    high = x.astype(BF16)
    return high, (x - high.astype(F32)).astype(BF16)


def stacked_rows(x):
    high = x.astype(BF16).astype(F32)
    return jnp.concatenate([high, x - high], axis=0).astype(BF16)


def three_way(x):
    high = x.astype(BF16).astype(F32)
    middle = (x - high).astype(BF16).astype(F32)
    return high, middle, x - high - middle


def element_loads(nc, lam_ref, table_ref, stiff_ref, mass_ref, dofs_ref, slab_ref, var_ref,
                  send_ref, slope_ref, mode_at, loads, matrices_here):
    ed, count = dofs_ref.shape
    lanes = table_ref.shape[1]
    cap = send_ref.shape[2]
    lam = lam_ref[0]
    dofs, slab, var = dofs_ref[...], slab_ref[...], var_ref[...]
    row_of = lax.shift_right_logical(dofs, 7) * nc + slab
    lane_of = jnp.bitwise_and(dofs, lanes - 1)
    chunks = count // lanes

    def look(step, found):
        found = list(found)
        for inner in range(8):
            r = step * 8 + inner
            row = jnp.broadcast_to(table_ref[pl.ds(r, 1), :], (ed, lanes))
            for c in range(chunks):
                at = slice(c * lanes, (c + 1) * lanes)
                taken = jnp.take_along_axis(row, lane_of[:, at], axis=1, mode="promise_in_bounds")
                found[c] = jnp.where(row_of[:, at] == r, taken, found[c])
        return tuple(found)

    found = lax.fori_loop(0, table_ref.shape[0] // 8, look, (jnp.zeros((ed, lanes), F32),) * chunks)
    for c in range(chunks):
        mode_at[:, c * lanes : (c + 1) * lanes] = found[c]
    modes = mode_at[...]
    matrices_here()
    for i in range(ed):
        operator = stiff_ref[i] - lam * mass_ref[i]
        loads[i : i + 1, :] = -jnp.sum(operator * modes, axis=0, keepdims=True)
    values = loads[...]
    quadratic = -jnp.sum(modes * values, axis=0, keepdims=True)
    padded = slope_ref.shape[1]
    matches = (lax.broadcasted_iota(jnp.int32, (padded, count), 0) == var).astype(F32).astype(BF16)
    terms = jnp.concatenate(list(three_way(quadratic)) + [jnp.zeros((5, count), F32)], axis=0).astype(BF16)
    nt = (((1,), (1,)), ((), ()))
    sums = lax.dot_general(terms, matches, nt, preferred_element_type=F32)
    slope_ref[...] = jnp.broadcast_to(jnp.sum(sums, axis=0, keepdims=True), slope_ref.shape)
    merged = jnp.zeros((ed, count), F32)
    for i in range(ed):
        merged = merged + jnp.where(dofs == dofs[i : i + 1, :], values[i : i + 1, :], 0.0)
    onehot = (lax.broadcasted_iota(jnp.int32, (nc, count), 0) == slab).astype(F32)
    earlier = lax.broadcasted_iota(jnp.int32, (count, count), 0) < lax.broadcasted_iota(jnp.int32, (count, count), 1)
    rank_all = jnp.dot(onehot.astype(BF16), earlier.astype(F32).astype(BF16), preferred_element_type=F32)
    rank = jnp.sum(onehot * rank_all, axis=0, keepdims=True).astype(jnp.int32)
    slot = slab * cap + rank
    high, middle, low = three_way(merged)
    coarse = lax.shift_right_logical(dofs, 4).astype(F32)
    fine = jnp.bitwise_and(dofs, 15).astype(F32)
    var_rows = jnp.concatenate([var.astype(F32), jnp.zeros((7, count), F32)], axis=0)
    data = jnp.concatenate([high, middle, low, coarse, fine, var_rows], axis=0).astype(BF16)
    for k in range(nc):
        place = (lax.broadcasted_iota(jnp.int32, (cap, count), 0) + k * cap == slot).astype(F32).astype(BF16)
        packed = lax.dot_general(data, place, nt, preferred_element_type=F32)
        send_ref[k, 0:ed, :] = (packed[0:ed] + packed[ed : 2 * ed]) + packed[2 * ed : 3 * ed]
        send_ref[k, ed : 2 * ed, :] = packed[3 * ed : 4 * ed] * 16.0 + packed[4 * ed : 5 * ed]
        send_ref[k, 2 * ed : 2 * ed + 8, :] = packed[5 * ed : 5 * ed + 8]


def solve_kernel(nc, nb, lam_ref, diag_ref, coup_ref, stiff_ref, emass_ref, dofs_ref, slab_ref, var_ref, mode_ref, mass_ref,
                 out_ref, slope_out, stiff, emass, mode_tile, mode_chain, mode_group, table, mode_at, loads, send_ref, got_ref, slope_ref,
                 dbuf, cbuf, dsplit, csplit, spread_ref, rpart, rbuf, sl_chain, sl_band, outer,
                 part, slots, piece, full, ybuf, xbuf,
                 el_sem, mc_send, mc_recv, mb_send, mb_recv, ex_send, ex_recv, mat, own_send, relay_send, slc_send, slc_recv, slb_send, slb_recv, r_send, r_recv, rp_send, rp_recv,
                 rs_send, rs_recv, ag_send, ag_recv, out_send, out_recv):
    me, band = lax.axis_index("chain"), lax.axis_index("band")
    x_len = nc // 2
    my_x, core = me // 2, lax.rem(me, 2)
    rows, width = part.shape
    cols = width // nb
    nvars = rpart.shape[0]
    sibling = 2 * my_x + 1 - core
    blocks = (dbuf, cbuf)
    nt = (((1,), (1,)), ((), ()))
    nn = (((1,), (0,)), ((), ()))

    def at_band(b):
        return pl.ds(pl.multiple_of(b * cols, cols), cols)

    side = math.isqrt(nb)
    hops = lambda r: min(r // side, side - r // side) + min(r % side, side - r % side)
    others = sorted(range(1, nb), key=lambda r: (-hops(r), r))
    band_z, band_y = band // side, lax.rem(band, side)

    def band_to(r):
        return lax.rem(band_z + r // side, side) * side + lax.rem(band_y + r % side, side)

    def band_from(r):
        return lax.rem(band_z + side - r // side, side) * side + lax.rem(band_y + side - r % side, side)

    def at_group(c):
        return pl.ds(pl.multiple_of(c * rows, 8), rows)

    def along_x(by):
        return 2 * lax.rem(my_x + by + x_len, x_len) + core

    def remote(src, dst, send, recv, chain, to_band):
        return pltpu.make_async_remote_copy(src_ref=src, dst_ref=dst, send_sem=send, recv_sem=recv,
                                            device_id=(chain, to_band), device_id_type=MESH)

    def each_block(which, work):
        if which == 0:
            work()
        else:
            pl.when(me != 0)(work)

    def own_load(which):
        return pltpu.make_async_copy((diag_ref, coup_ref)[which], blocks[which].at[me], mat.at[which, me])

    def own_copy(which, i):
        to = (along_x(1), along_x(-1), sibling)[i]
        return remote((diag_ref, coup_ref)[which], blocks[which].at[me], own_send.at[which, i], mat.at[which, me], to, band)

    stiff_load = pltpu.make_async_copy(stiff_ref, stiff, el_sem.at[0])
    emass_load = pltpu.make_async_copy(emass_ref, emass, el_sem.at[1])
    stiff_load.start()
    emass_load.start()
    for which in range(2):
        each_block(which, lambda which=which: own_load(which).start())
    line = lax.broadcasted_iota(jnp.int32, mode_tile.shape, 0)
    mode_tile[...] = jnp.where(line == 0, mode_ref[...], jnp.where(line == 1, mass_ref[...], 0.0))

    barrier = pltpu.get_barrier_semaphore()
    for r in range(1, nb):
        pl.semaphore_signal(barrier, inc=1, device_id=(me, band_to(r)), device_id_type=MESH)
    for r in range(1, nc):
        pl.semaphore_signal(barrier, inc=1, device_id=(lax.rem(me + r, nc), band), device_id_type=MESH)
    pl.semaphore_wait(barrier, nb + nc - 2)

    def mode_chain_copy(to, source):
        return remote(mode_tile, mode_chain.at[source], mc_send.at[to], mc_recv.at[source], to, band)

    for r in range(1, nc):
        mode_chain_copy(lax.rem(me + r, nc), me).start()
    mode_chain[me] = mode_tile[...]

    def send_own(which):
        for i in range(3):
            own_copy(which, i).start()

    pl.when(me != 1)(lambda: send_own(0))
    pl.when(me == 1)(lambda: send_own(1))
    for r in range(1, nc):
        mode_chain_copy(me, lax.rem(me + r, nc)).wait_recv()
    line = lax.broadcasted_iota(jnp.int32, (nc, cols), 0)
    whole = jnp.zeros((nc, cols), F32)
    for c in range(nc):
        whole = jnp.where(line == c, mode_chain[c, 0:1, :], whole)
    mode_group[...] = whole

    def at_rows(b):
        return table.at[pl.ds(pl.multiple_of(b * nc, 8), nc), :]

    def mode_band_copy(r):
        to = band_to(r)
        return remote(mode_group, at_rows(band), mb_send.at[r], mb_recv.at[r], me, to)

    def mode_band_arrival(r):
        source = band_from(r)
        return remote(mode_group, at_rows(source), mb_send.at[r], mb_recv.at[r], me, source)

    for r in others:
        mode_band_copy(r).start()
    table[pl.ds(pl.multiple_of(band * nc, 8), nc), :] = whole
    for r in range(1, nb):
        mode_band_arrival(r).wait_recv()

    def matrices_here():
        stiff_load.wait()
        emass_load.wait()

    element_loads(nc, lam_ref, table, stiff, emass, dofs_ref, slab_ref, var_ref, send_ref, slope_ref, mode_at, loads, matrices_here)

    def relay_on(which, by):
        slab = along_x(-by)
        block = blocks[which].at[slab]
        return remote(block, block, relay_send.at[which, by, 0], mat.at[which, slab], sibling, band)

    def relay_further(which, by):
        slab = along_x(-by)
        block = blocks[which].at[slab]
        return remote(block, block, relay_send.at[which, by, 1], mat.at[which, slab], along_x(1 if by == 1 else -1), band)

    def each_relayed(which, by, work):
        if which == 0:
            work()
        else:
            pl.when(along_x(-by) != 0)(work)

    def forwards(by):
        return {1: core == 0, 3: core == 1}[by]

    def relay(which, by):
        slab = along_x(-by)

        def work():
            pltpu.make_async_copy(blocks[which].at[slab], blocks[which].at[slab], mat.at[which, slab]).wait()
            if by != 2:
                pl.when(forwards(by))(lambda: relay_further(which, by).start())
            relay_on(which, by).start()

        each_relayed(which, by, work)

    def relay_farthest(which, k):
        pl.when(k == along_x(2))(lambda: relay(which, 2))

    def element_copy(to, source):
        return remote(send_ref.at[to], got_ref.at[source], ex_send.at[to], ex_recv.at[source], to, band)

    def slope_chain_copy(to, source):
        return remote(slope_ref, sl_chain.at[source], slc_send.at[to], slc_recv.at[source], to, band)

    for r in range(1, nc):
        element_copy(lax.rem(me + r, nc), me).start()
        slope_chain_copy(lax.rem(me + r, nc), me).start()
    sl_chain[me] = slope_ref[...]
    got_ref[me] = send_ref[me]
    pl.when(core == 0)(lambda: relay(0, 1))

    @pl.when(core == 1)
    def _():
        pl.when(along_x(1) != 1)(lambda: relay(0, 3))
        pl.when(along_x(1) == 1)(lambda: relay(1, 3))

    pl.when(me == 1)(lambda: send_own(0))
    pl.when((me != 0) & (me != 1))(lambda: send_own(1))
    for r in range(1, nc):
        element_copy(me, lax.rem(me + r, nc)).wait_recv()

    cap = got_ref.shape[2]
    ed = (got_ref.shape[1] - 8) // 2
    block = spread_ref.shape[0]
    lines = 128
    base = lax.broadcasted_iota(jnp.int32, (lines, cap), 0)
    variable = lax.broadcasted_iota(jnp.int32, (nvars, cap), 0)
    matches = [(variable == got_ref[s, 2 * ed : 2 * ed + 1, :].astype(jnp.int32)).astype(F32).astype(BF16) for s in range(nc)]
    matches = jnp.concatenate(matches + matches, axis=1)

    def rhs_copy(to, source):
        return remote(rpart.at[at_group(to), :], rbuf.at[source], r_send.at[to], r_recv.at[source], to, band)

    def rhs_part_copy(to, n):
        at = pl.ds(pl.multiple_of(n * block, block), block)
        return remote(rpart.at[at_group(to), at], rbuf.at[0, :, at], rp_send.at[to, n], rp_recv.at[n], to, band)

    def send_rhs():
        for r in range(1, nc):
            rhs_copy(lax.rem(me + r, nc), me).start()

    def rhs_wait(k):
        pl.when(k != me)(lambda: rhs_copy(me, k).wait_recv())

    def one_block(n, carry):
        def one_source(s, inner):
            values = got_ref[s, 0:ed, :]
            dofs = got_ref[s, ed : 2 * ed, :].astype(jnp.int32) - n * block
            for half in range(block // lines):
                total = jnp.zeros((lines, cap), F32)
                for i in range(ed):
                    hit = base == dofs[i : i + 1, :] - half * lines
                    total = jnp.where(hit, values[i : i + 1, :], total)
                high = total.astype(BF16)
                at = pl.ds(pl.multiple_of(s * cap, cap), cap)
                spread_ref[half * lines : (half + 1) * lines, at] = high
                at = pl.ds(pl.multiple_of((s + nc) * cap, cap), cap)
                spread_ref[half * lines : (half + 1) * lines, at] = (total - high.astype(F32)).astype(BF16)
            return inner

        lax.fori_loop(0, nc, one_source, 0)
        at = pl.ds(pl.multiple_of(n * block, block), block)
        rpart[:, at] = lax.dot_general(matches, spread_ref[...], nt, preferred_element_type=F32)

        @pl.when(me == 0)
        def _():
            for r in range(1, nc):
                rhs_part_copy(r, n).start()

        return carry

    lax.fori_loop(0, width // block, one_block, 0)

    rbuf[me] = rpart[at_group(me), :]

    for r in range(1, nc):
        slope_chain_copy(me, lax.rem(me + r, nc)).wait_recv()
    total = sl_chain[0]
    for c in range(1, nc):
        total = total + sl_chain[c]

    def slope_band_copy(r):
        to = band_to(r)
        return remote(sl_band.at[band], sl_band.at[band], slb_send.at[r], slb_recv.at[r], me, to)

    def slope_band_arrival(r):
        source = band_from(r)
        return remote(sl_band.at[source], sl_band.at[source], slb_send.at[r], slb_recv.at[r], me, source)

    sl_band[band] = total
    for r in others:
        slope_band_copy(r).start()

    def slope_term():
        for r in range(1, nb):
            slope_band_arrival(r).wait_recv()
        total = sl_band[0]
        for b in range(1, nb):
            total = total + sl_band[b]
        slope_out[...] = total[0:1, :nvars]
        line = lax.broadcasted_iota(jnp.int32, total.shape, 0)
        high, middle, low = three_way(total)
        slope_terms = jnp.where((line == 0) | (line == 3) | (line == 5), high, 0.0)
        slope_terms = jnp.where((line == 1) | (line == 4), middle, jnp.where(line == 2, low, slope_terms))
        line = lax.broadcasted_iota(jnp.int32, (8, cols), 0)
        for k in range(nc):
            high, middle, low = three_way(jnp.broadcast_to(mode_chain[k, 1:2, :], (8, cols)))
            mass_terms = jnp.where(line < 3, high, jnp.where(line < 5, middle, jnp.where(line == 5, low, 0.0)))
            outer[k] = lax.dot_general(slope_terms.astype(BF16), mass_terms.astype(BF16), (((0,), (0,)), ((), ())), preferred_element_type=F32)

    @pl.when(core == 0)
    def _():
        relay(1, 1)
        relay(0, 3)
        relay(1, 3)

    @pl.when(core == 1)
    def _():
        pl.when(along_x(1) != 1)(lambda: relay(1, 3))
        pl.when(along_x(1) == 1)(lambda: relay(0, 3))
        relay(0, 1)
        relay(1, 1)


    def rs_copy(r):
        to = band_to(r)
        return remote(part.at[:, at_band(to)], slots.at[r], rs_send.at[r], rs_recv.at[r], me, to)

    def ag_copy(r):
        to = band_to(r)
        return remote(piece, full.at[:, at_band(band)], ag_send.at[r], ag_recv.at[r], me, to)

    def ag_arrival(r):
        source = band_from(r)
        return remote(piece, full.at[:, at_band(source)], ag_send.at[r], ag_recv.at[r], me, source)

    def reduce_start():
        for r in others:
            rs_copy(r).start()

    def reduce_end(own):
        total = own
        for r in reversed(others):
            rs_copy(r).wait_recv()
            total = total + slots[r]
        return total

    def reduce_sent():
        for r in others:
            rs_copy(r).wait_send()

    def gather_start(value):
        piece[...] = value
        for r in others:
            ag_copy(r).start()
        full[:, at_band(band)] = value

    def gather_end():
        for r in reversed(others):
            ag_arrival(r).wait_recv()

    def gather_sent():
        for r in others:
            ag_copy(r).wait_send()

    def block_wait(which, k):
        @pl.when((lax.rem(k, 2) != core) | (k == me))
        def _():
            pltpu.make_async_copy(blocks[which].at[k], blocks[which].at[k], mat.at[which, k]).wait()

    def split_diag(k):
        block_wait(0, k)
        high, low = split2(dbuf[k])
        dsplit[k, 0:cols, :] = high
        dsplit[k, cols : 2 * cols, :] = low

    def split_coup(k):
        block_wait(1, k)
        high, low = split2(cbuf[k])
        csplit[k, :, 0:cols] = high
        csplit[k, :, cols : 2 * cols] = low

    def narrow(value, weights, dims):
        wide = lax.dot_general(stacked_rows(value), weights, dims, preferred_element_type=F32)
        return (wide[:rows, :cols] + wide[:rows, cols:]) + (wide[rows:, :cols] + wide[rows:, cols:])

    def spread(value, weights, dims):
        both = stacked_rows(value)
        both = jnp.concatenate([both, both], axis=1)
        wide = lax.dot_general(both, weights, dims, preferred_element_type=F32)
        return wide[:rows] + wide[rows:]

    @pl.when(me != 0)
    def _():
        for n in range(width // block):
            rhs_part_copy(me, n).wait_recv()

    part[...] = rbuf[0]
    pl.when(me == 1)(send_rhs)

    def forward(k, carry):
        reduce_start()
        pl.when(me == k + 2)(send_rhs)
        pl.when(k > 0)(gather_sent)
        pl.when(k == 0)(lambda: relay_farthest(0, 0))
        pl.when(k == 0)(slope_term)
        relay_farthest(0, k + 1)
        relay_farthest(1, k + 1)
        split_diag(k)
        gather_start(reduce_end(part[:, at_band(band)] + outer[k, at_group(me), :]))
        reduce_sent()

        @pl.when(k + 1 < nc)
        def _():
            split_coup(k + 1)

        gather_end()
        solved = narrow(full[...], dsplit[k], nt)
        ybuf[k] = solved

        @pl.when(k + 1 < nc)
        def _():
            rhs_wait(k + 1)
            part[...] = rbuf[k + 1] - spread(solved, csplit[k + 1], nt)

        return carry

    lax.fori_loop(0, nc, forward, 0)

    def out_copy(k, source):
        return remote(xbuf.at[k], out_ref.at[at_group(source), :], out_send.at[k], out_recv.at[source], k, band)

    def backward(step, coupled):
        k = nc - 1 - step
        part[...] = spread(ybuf[k] - coupled, dsplit[k], nn)
        reduce_start()
        gather_sent()
        total = reduce_end(part[:, at_band(band)])
        gather_start(total)
        reduce_sent()
        xbuf[k] = total

        @pl.when(k != me)
        def _():
            out_copy(k, me).start()

        @pl.when(k == me)
        def _():
            out_ref[at_group(me), :] = total

        gather_end()
        return narrow(full[...], csplit[k], nn)

    coupled = lax.fori_loop(0, nc - 1, backward, jnp.zeros((rows, cols), F32))
    part[...] = spread(ybuf[0] - coupled, dsplit[0], nn)
    reduce_start()
    gather_sent()
    total = reduce_end(part[:, at_band(band)])
    xbuf[0] = total
    pl.when(me != 0)(lambda: out_copy(0, me).start())

    @pl.when(me == 0)
    def _():
        out_ref[at_group(0), :] = total

    for r in range(1, nc):
        other = lax.rem(me + r, nc)
        out_copy(other, me).wait_send()
        out_copy(me, other).wait_recv()
        pl.when(me != 0)(lambda other=other: rhs_copy(other, me).wait_send())

        @pl.when(me == 0)
        def _():
            for n in range(width // block):
                rhs_part_copy(other, n).wait_send()

        slope_chain_copy(other, me).wait_send()
        mode_chain_copy(other, me).wait_send()
        element_copy(other, me).wait_send()
    reduce_sent()
    for r in range(1, nb):
        slope_band_copy(r).wait_send()
        mode_band_copy(r).wait_send()

    def sent(which):
        for i in range(3):
            own_copy(which, i).wait_send()

    for which in range(2):
        each_block(which, functools.partial(sent, which))
        for by in (1, 2, 3):

            def relayed(which=which, by=by):
                relay_on(which, by).wait_send()
                if by != 2:
                    pl.when(forwards(by))(lambda: relay_further(which, by).wait_send())

            each_relayed(which, by, relayed)


def on_device(nc, nb, diag_inverse, coupling, elem_stiff, elem_mass, elem_dofs, elem_slab, elem_var, mode, mass_mode, eigenvalue):
    band = lax.axis_index("band")
    cols, width = diag_inverse.shape
    ed, count = elem_dofs.shape
    cap = count // 4
    rows = VARS // nc
    padded = 256
    vmem = pl.BlockSpec(memory_space=pltpu.VMEM)
    anywhere = pl.BlockSpec(memory_space=pl.ANY)
    own_mass = lax.dynamic_slice_in_dim(mass_mode, band * cols, cols)[None, :]
    dma = pltpu.SemaphoreType.DMA
    eigvec_slope, eigval_slope = pl.pallas_call(
        functools.partial(solve_kernel, nc, nb),
        out_shape=(jax.ShapeDtypeStruct((VARS, cols), F32), jax.ShapeDtypeStruct((1, VARS), F32)),
        in_specs=[pl.BlockSpec(memory_space=pltpu.SMEM)] + [anywhere] * 4 + [vmem] * 5,
        out_specs=(vmem, vmem),
        scratch_shapes=[
            pltpu.VMEM((ed, ed, count), F32),
            pltpu.VMEM((ed, ed, count), F32),
            pltpu.VMEM((8, cols), F32),
            pltpu.VMEM((nc, 8, cols), F32),
            pltpu.VMEM((nc, cols), F32),
            pltpu.VMEM((nc * nb, cols), F32),
            pltpu.VMEM((ed, count), F32),
            pltpu.VMEM((ed, count), F32),
            pltpu.VMEM((nc, 2 * ed + 8, cap), F32),
            pltpu.VMEM((nc, 2 * ed + 8, cap), F32),
            pltpu.VMEM((8, padded), F32),
            pltpu.VMEM((nc, cols, width), F32),
            pltpu.VMEM((nc, width, cols), F32),
            pltpu.VMEM((nc, 2 * cols, width), BF16),
            pltpu.VMEM((nc, width, 2 * cols), BF16),
            pltpu.VMEM((256, 2 * nc * cap), BF16),
            pltpu.VMEM((VARS, width), F32),
            pltpu.VMEM((nc, rows, width), F32),
            pltpu.VMEM((nc, 8, padded), F32),
            pltpu.VMEM((nb, 8, padded), F32),
            pltpu.VMEM((nc, padded, cols), F32),
            pltpu.VMEM((rows, width), F32),
            pltpu.VMEM((nb, rows, cols), F32),
            pltpu.VMEM((rows, cols), F32),
            pltpu.VMEM((rows, width), F32),
            pltpu.VMEM((nc, rows, cols), F32),
            pltpu.VMEM((nc, rows, cols), F32),
            dma((2,)), dma((nc,)), dma((nc,)), dma((nb,)), dma((nb,)), dma((nc,)), dma((nc,)),
            dma((2, nc)), dma((2, 3)), dma((2, 4, 2)),
            dma((nc,)), dma((nc,)), dma((nb,)), dma((nb,)), dma((nc,)), dma((nc,)),
            dma((nc, 8)), dma((8,)),
            dma((nb,)), dma((nb,)), dma((nb,)), dma((nb,)), dma((nc,)), dma((nc,)),
        ],
        compiler_params=pltpu.CompilerParams(collective_id=0, has_side_effects=True, vmem_limit_bytes=52 * 1024 * 1024),
        cost_estimate=pl.CostEstimate(flops=10**10, bytes_accessed=10**8, transcendentals=0),
        name="solve",
    )(eigenvalue, diag_inverse, coupling, elem_stiff, elem_mass, elem_dofs, elem_slab.reshape(1, count),
      elem_var.reshape(1, count), mode[None, :], own_mass)
    return eigvec_slope, eigval_slope.reshape(VARS)


def solution(mesh):
    nc, nb = mesh.shape["chain"], mesh.shape["band"]
    in_specs = (
        P(("chain", "band"), None),
        P("chain", "band"),
        P(None, None, ("chain", "band")),
        P(None, None, ("chain", "band")),
        P(None, ("chain", "band")),
        P(("chain", "band"), None),
        P(("chain", "band")),
        P(("chain", "band")),
        P("chain"),
        P(),
    )
    out_specs = (P(None, ("chain", "band")), P())
    return jax.shard_map(functools.partial(on_device, nc, nb), mesh=mesh, in_specs=in_specs, out_specs=out_specs, check_vma=False)
```

```python
import functools
import math

import jax
import jax.numpy as jnp
from jax import lax
from jax.experimental import pallas as pl
from jax.experimental.pallas import tpu as pltpu
from jax.sharding import PartitionSpec as P

MESH = pl.DeviceIdType.MESH
F32 = jnp.float32
BF16 = jnp.bfloat16
VARS = 192


def split2(x):
    high = x.astype(BF16)
    return high, (x - high.astype(F32)).astype(BF16)


def stacked_rows(x):
    high = x.astype(BF16).astype(F32)
    return jnp.concatenate([high, x - high], axis=0).astype(BF16)


def three_way(x):
    high = x.astype(BF16).astype(F32)
    middle = (x - high).astype(BF16).astype(F32)
    return high, middle, x - high - middle


def element_loads(nc, lam_ref, table_ref, stiff_ref, mass_ref, dofs_ref, slab_ref, var_ref,
                  send_ref, slope_ref, mode_at, loads, matrices_here):
    ed, count = dofs_ref.shape
    lanes = table_ref.shape[1]
    cap = send_ref.shape[2]
    lam = lam_ref[0]
    dofs, slab, var = dofs_ref[...], slab_ref[...], var_ref[...]
    row_of = lax.shift_right_logical(dofs, 7) * nc + slab
    lane_of = jnp.bitwise_and(dofs, lanes - 1)
    chunks = count // lanes

    def look(step, found):
        found = list(found)
        for inner in range(8):
            r = step * 8 + inner
            row = jnp.broadcast_to(table_ref[pl.ds(r, 1), :], (ed, lanes))
            for c in range(chunks):
                at = slice(c * lanes, (c + 1) * lanes)
                taken = jnp.take_along_axis(row, lane_of[:, at], axis=1, mode="promise_in_bounds")
                found[c] = jnp.where(row_of[:, at] == r, taken, found[c])
        return tuple(found)

    found = lax.fori_loop(0, table_ref.shape[0] // 8, look, (jnp.zeros((ed, lanes), F32),) * chunks)
    for c in range(chunks):
        mode_at[:, c * lanes : (c + 1) * lanes] = found[c]
    modes = mode_at[...]
    matrices_here()
    for i in range(ed):
        operator = stiff_ref[i] - lam * mass_ref[i]
        loads[i : i + 1, :] = -jnp.sum(operator * modes, axis=0, keepdims=True)
    values = loads[...]
    quadratic = -jnp.sum(modes * values, axis=0, keepdims=True)
    padded = slope_ref.shape[1]
    matches = (lax.broadcasted_iota(jnp.int32, (padded, count), 0) == var).astype(F32).astype(BF16)
    terms = jnp.concatenate(list(three_way(quadratic)) + [jnp.zeros((5, count), F32)], axis=0).astype(BF16)
    nt = (((1,), (1,)), ((), ()))
    sums = lax.dot_general(terms, matches, nt, preferred_element_type=F32)
    slope_ref[...] = jnp.broadcast_to(jnp.sum(sums, axis=0, keepdims=True), slope_ref.shape)
    merged = jnp.zeros((ed, count), F32)
    for i in range(ed):
        merged = merged + jnp.where(dofs == dofs[i : i + 1, :], values[i : i + 1, :], 0.0)
    onehot = (lax.broadcasted_iota(jnp.int32, (nc, count), 0) == slab).astype(F32)
    earlier = lax.broadcasted_iota(jnp.int32, (count, count), 0) < lax.broadcasted_iota(jnp.int32, (count, count), 1)
    rank_all = jnp.dot(onehot.astype(BF16), earlier.astype(F32).astype(BF16), preferred_element_type=F32)
    rank = jnp.sum(onehot * rank_all, axis=0, keepdims=True).astype(jnp.int32)
    slot = slab * cap + rank
    high, middle, low = three_way(merged)
    coarse = lax.shift_right_logical(dofs, 4).astype(F32)
    fine = jnp.bitwise_and(dofs, 15).astype(F32)
    var_rows = jnp.concatenate([var.astype(F32), jnp.zeros((7, count), F32)], axis=0)
    data = jnp.concatenate([high, middle, low, coarse, fine, var_rows], axis=0).astype(BF16)
    for k in range(nc):
        place = (lax.broadcasted_iota(jnp.int32, (cap, count), 0) + k * cap == slot).astype(F32).astype(BF16)
        packed = lax.dot_general(data, place, nt, preferred_element_type=F32)
        send_ref[k, 0:ed, :] = (packed[0:ed] + packed[ed : 2 * ed]) + packed[2 * ed : 3 * ed]
        send_ref[k, ed : 2 * ed, :] = packed[3 * ed : 4 * ed] * 16.0 + packed[4 * ed : 5 * ed]
        send_ref[k, 2 * ed : 2 * ed + 8, :] = packed[5 * ed : 5 * ed + 8]


def solve_kernel(nc, nb, lam_ref, diag_ref, coup_ref, stiff_ref, emass_ref, dofs_in, slab_in, var_in, mode_in, mass_in,
                 out_ref, slope_out, dofs_ref, slab_ref, var_ref, mode_ref, mass_ref, stiff, emass, mode_tile, mode_chain, mode_group, table, mode_at, loads, send_ref, got_ref, slope_ref,
                 dbuf, cbuf, dsplit, csplit, spread_ref, rpart, rslots, rsum, rpiece, sl_chain, sl_band, outer,
                 part, slots, piece, full, ybuf, xbuf,
                 el_sem, mc_send, mc_recv, mb_send, mb_recv, ex_send, ex_recv, mat, own_send, relay_send, slc_send, slc_recv, slb_send, slb_recv, r_send, r_recv, rq_send, rq_recv,
                 rs_send, rs_recv, ag_send, ag_recv, out_send, out_recv):
    me, band = lax.axis_index("chain"), lax.axis_index("band")
    x_len = nc // 2
    my_x, core = me // 2, lax.rem(me, 2)
    rows, width = part.shape
    cols = width // nb
    nvars = rpart.shape[0]
    sibling = 2 * my_x + 1 - core
    blocks = (dbuf, cbuf)
    nt = (((1,), (1,)), ((), ()))
    nn = (((1,), (0,)), ((), ()))

    def at_band(b):
        return pl.ds(pl.multiple_of(b * cols, cols), cols)

    side = math.isqrt(nb)
    hops = lambda r: min(r // side, side - r // side) + min(r % side, side - r % side)
    others = sorted(range(1, nb), key=lambda r: (-hops(r), r))
    band_z, band_y = band // side, lax.rem(band, side)

    def band_to(r):
        return lax.rem(band_z + r // side, side) * side + lax.rem(band_y + r % side, side)

    def band_from(r):
        return lax.rem(band_z + side - r // side, side) * side + lax.rem(band_y + side - r % side, side)

    def at_group(c):
        return pl.ds(pl.multiple_of(c * rows, 8), rows)

    def along_x(by):
        return 2 * lax.rem(my_x + by + x_len, x_len) + core

    def remote(src, dst, send, recv, chain, to_band):
        return pltpu.make_async_remote_copy(src_ref=src, dst_ref=dst, send_sem=send, recv_sem=recv,
                                            device_id=(chain, to_band), device_id_type=MESH)

    def each_block(which, work):
        if which == 0:
            work()
        else:
            pl.when(me != 0)(work)

    def own_load(which):
        return pltpu.make_async_copy((diag_ref, coup_ref)[which], blocks[which].at[me], mat.at[which, me])

    def own_copy(which, i):
        to = (along_x(1), along_x(-1), sibling)[i]
        return remote((diag_ref, coup_ref)[which], blocks[which].at[me], own_send.at[which, i], mat.at[which, me], to, band)

    small = ((mode_in, mode_ref), (mass_in, mass_ref), (dofs_in, dofs_ref), (slab_in, slab_ref), (var_in, var_ref))
    small_loads = [pltpu.make_async_copy(src, dst, el_sem.at[2 + i]) for i, (src, dst) in enumerate(small)]
    for load in small_loads:
        load.start()
    stiff_load = pltpu.make_async_copy(stiff_ref, stiff, el_sem.at[0])
    emass_load = pltpu.make_async_copy(emass_ref, emass, el_sem.at[1])
    stiff_load.start()
    emass_load.start()
    for which in range(2):
        each_block(which, lambda which=which: own_load(which).start())
    for load in small_loads:
        load.wait()
    line = lax.broadcasted_iota(jnp.int32, mode_tile.shape, 0)
    mode_tile[...] = jnp.where(line == 0, mode_ref[...], jnp.where(line == 1, mass_ref[...], 0.0))

    barrier = pltpu.get_barrier_semaphore()
    for r in range(1, nb):
        pl.semaphore_signal(barrier, inc=1, device_id=(me, band_to(r)), device_id_type=MESH)
    for r in range(1, nc):
        pl.semaphore_signal(barrier, inc=1, device_id=(lax.rem(me + r, nc), band), device_id_type=MESH)
    pl.semaphore_wait(barrier, nb + nc - 2)

    def send_own(which):
        for i in range(3):
            own_copy(which, i).start()

    def relay_on(which, by):
        slab = along_x(-by)
        block = blocks[which].at[slab]
        return remote(block, block, relay_send.at[which, by, 0], mat.at[which, slab], sibling, band)

    def relay_further(which, by):
        slab = along_x(-by)
        block = blocks[which].at[slab]
        return remote(block, block, relay_send.at[which, by, 1], mat.at[which, slab], along_x(1 if by == 1 else -1), band)

    def each_relayed(which, by, work):
        if which == 0:
            work()
        else:
            pl.when(along_x(-by) != 0)(work)

    def forwards(by):
        return {1: core == 0, 3: core == 1}[by]

    def relay(which, by):
        slab = along_x(-by)

        def work():
            pltpu.make_async_copy(blocks[which].at[slab], blocks[which].at[slab], mat.at[which, slab]).wait()
            if by != 2:
                pl.when(forwards(by))(lambda: relay_further(which, by).start())
            relay_on(which, by).start()

        each_relayed(which, by, work)

    def relay_farthest(which, k):
        pl.when(k == along_x(2))(lambda: relay(which, 2))

    def first_sends():
        pl.when(me != 1)(lambda: send_own(0))
        pl.when(me == 1)(lambda: send_own(1))

    def second_sends():
        pl.when(me == 1)(lambda: send_own(0))
        pl.when((me != 0) & (me != 1))(lambda: send_own(1))

    def first_relays():
        pl.when(core == 0)(lambda: relay(0, 1))

        @pl.when(core == 1)
        def _():
            pl.when(along_x(1) != 1)(lambda: relay(0, 3))
            pl.when(along_x(1) == 1)(lambda: relay(1, 3))

    def second_relays():
        @pl.when(core == 0)
        def _():
            relay(1, 1)
            relay(0, 3)
            relay(1, 3)

        @pl.when(core == 1)
        def _():
            pl.when(along_x(1) != 1)(lambda: relay(1, 3))
            pl.when(along_x(1) == 1)(lambda: relay(0, 3))
            relay(0, 1)
            relay(1, 1)

    def mode_chain_copy(to, source):
        return remote(mode_tile, mode_chain.at[source], mc_send.at[to], mc_recv.at[source], to, band)

    for r in range(1, nc):
        mode_chain_copy(lax.rem(me + r, nc), me).start()
    mode_chain[me] = mode_tile[...]

    first_sends()
    for r in range(1, nc):
        mode_chain_copy(me, lax.rem(me + r, nc)).wait_recv()
    line = lax.broadcasted_iota(jnp.int32, (nc, cols), 0)
    whole = jnp.zeros((nc, cols), F32)
    for c in range(nc):
        whole = jnp.where(line == c, mode_chain[c, 0:1, :], whole)
    mode_group[...] = whole

    def at_rows(b):
        return table.at[pl.ds(pl.multiple_of(b * nc, 8), nc), :]

    def mode_band_copy(r):
        to = band_to(r)
        return remote(mode_group, at_rows(band), mb_send.at[r], mb_recv.at[r], me, to)

    def mode_band_arrival(r):
        source = band_from(r)
        return remote(mode_group, at_rows(source), mb_send.at[r], mb_recv.at[r], me, source)

    for r in others:
        mode_band_copy(r).start()
    table[pl.ds(pl.multiple_of(band * nc, 8), nc), :] = whole
    for r in range(1, nb):
        mode_band_arrival(r).wait_recv()

    def matrices_here():
        stiff_load.wait()
        emass_load.wait()

    element_loads(nc, lam_ref, table, stiff, emass, dofs_ref, slab_ref, var_ref, send_ref, slope_ref, mode_at, loads, matrices_here)

    def element_copy(to, source):
        return remote(send_ref.at[to], got_ref.at[source], ex_send.at[to], ex_recv.at[source], to, band)

    def slope_chain_copy(to, source):
        return remote(slope_ref, sl_chain.at[source], slc_send.at[to], slc_recv.at[source], to, band)

    for r in range(1, nc):
        element_copy(lax.rem(me + r, nc), me).start()
        slope_chain_copy(lax.rem(me + r, nc), me).start()
    sl_chain[me] = slope_ref[...]
    got_ref[me] = send_ref[me]
    first_relays()
    second_sends()
    for r in range(1, nc):
        element_copy(me, lax.rem(me + r, nc)).wait_recv()

    for r in range(1, nc):
        slope_chain_copy(me, lax.rem(me + r, nc)).wait_recv()
    total = sl_chain[0]
    for c in range(1, nc):
        total = total + sl_chain[c]

    def slope_band_copy(r):
        to = band_to(r)
        return remote(sl_band.at[band], sl_band.at[band], slb_send.at[r], slb_recv.at[r], me, to)

    def slope_band_arrival(r):
        source = band_from(r)
        return remote(sl_band.at[source], sl_band.at[source], slb_send.at[r], slb_recv.at[r], me, source)

    sl_band[band] = total
    for r in others:
        slope_band_copy(r).start()

    def slope_term():
        for r in others:
            slope_band_arrival(r).wait_recv()
        total = sl_band[0]
        for b in range(1, nb):
            total = total + sl_band[b]
        slope_out[...] = total[0:1, :nvars]
        line = lax.broadcasted_iota(jnp.int32, total.shape, 0)
        high, middle, low = three_way(total)
        slope_terms = jnp.where((line == 0) | (line == 3) | (line == 5), high, 0.0)
        slope_terms = jnp.where((line == 1) | (line == 4), middle, jnp.where(line == 2, low, slope_terms))
        line = lax.broadcasted_iota(jnp.int32, (8, cols), 0)
        for k in range(nc):
            high, middle, low = three_way(jnp.broadcast_to(mode_chain[k, 1:2, :], (8, cols)))
            mass_terms = jnp.where(line < 3, high, jnp.where(line < 5, middle, jnp.where(line == 5, low, 0.0)))
            outer[k] = lax.dot_general(slope_terms.astype(BF16), mass_terms.astype(BF16), (((0,), (0,)), ((), ())), preferred_element_type=F32)

    cap = got_ref.shape[2]
    ed = (got_ref.shape[1] - 8) // 2
    block = spread_ref.shape[0]
    lines = 256
    base = lax.broadcasted_iota(jnp.int32, (lines, cap), 0).astype(F32).astype(BF16)
    variable = lax.broadcasted_iota(jnp.int32, (nvars, cap), 0)
    matches = [(variable == got_ref[s, 2 * ed : 2 * ed + 1, :].astype(jnp.int32)).astype(F32).astype(BF16) for s in range(nc)]
    matches = jnp.concatenate(matches + matches, axis=1)

    def band_copy(to, source):
        return remote(rpart.at[:, at_band(to)], rslots.at[source], rq_send.at[to], rq_recv.at[source], me, to)

    per_block = block // cols

    def one_block(step, carry):
        n = lax.rem(step + 1 + band // per_block, width // block)

        def one_source(s, inner):
            values = got_ref[s, 0:ed, :]
            high = values.astype(BF16)
            low = (values - high.astype(F32)).astype(BF16)
            dofs = got_ref[s, ed : 2 * ed, :].astype(jnp.int32) - n * block
            for part_no in range(block // lines):
                shifted = dofs - part_no * lines
                shifted = jnp.where((shifted >= 0) & (shifted < lines), shifted, -1)
                place = shifted.astype(F32).astype(BF16)
                total_high = jnp.zeros((lines, cap), BF16)
                total_low = jnp.zeros((lines, cap), BF16)
                for i in range(ed):
                    hit = base == place[i : i + 1, :]
                    total_high = jnp.where(hit, high[i : i + 1, :], total_high)
                    total_low = jnp.where(hit, low[i : i + 1, :], total_low)
                at = pl.ds(pl.multiple_of(s * cap, cap), cap)
                spread_ref[part_no * lines : (part_no + 1) * lines, at] = total_high
                at = pl.ds(pl.multiple_of((s + nc) * cap, cap), cap)
                spread_ref[part_no * lines : (part_no + 1) * lines, at] = total_low
            return inner

        lax.fori_loop(0, nc, one_source, 0)
        at = pl.ds(pl.multiple_of(n * block, block), block)
        rpart[:, at] = lax.dot_general(matches, spread_ref[...], nt, preferred_element_type=F32)

        for j in range(per_block):
            to = n * per_block + j
            pl.when(to != band)(lambda to=to: band_copy(to, band).start())

        return carry

    lax.fori_loop(0, width // block, one_block, 0)

    slope_term()
    total = rpart[:, at_band(band)]
    for r in others:
        band_copy(band, band_from(r)).wait_recv()
        total = total + rslots[band_from(r)]
    rsum[...] = total

    def rhs_copy(to, source):
        return remote(rsum.at[at_group(to), :], rpiece.at[source], r_send.at[to], r_recv.at[source], to, band)

    for r in range(1, nc):
        rhs_copy(lax.rem(me + r, nc), me).start()
    rpiece[me] = rsum[at_group(me), :]

    def rhs_wait(k):
        pl.when(k != me)(lambda: rhs_copy(me, k).wait_recv())

    second_relays()

    def rs_copy(r):
        to = band_to(r)
        return remote(part.at[:, at_band(to)], slots.at[r], rs_send.at[r], rs_recv.at[r], me, to)

    def ag_copy(r):
        to = band_to(r)
        return remote(piece, full.at[:, at_band(band)], ag_send.at[r], ag_recv.at[r], me, to)

    def ag_arrival(r):
        source = band_from(r)
        return remote(piece, full.at[:, at_band(source)], ag_send.at[r], ag_recv.at[r], me, source)

    def reduce_start():
        for r in others:
            rs_copy(r).start()

    def reduce_end(own):
        total = own
        for r in reversed(others):
            rs_copy(r).wait_recv()
            total = total + slots[r]
        return total

    def reduce_sent():
        for r in others:
            rs_copy(r).wait_send()

    def gather_start(value):
        piece[...] = value
        for r in others:
            ag_copy(r).start()
        full[:, at_band(band)] = value

    def gather_end():
        for r in reversed(others):
            ag_arrival(r).wait_recv()

    def gather_sent():
        for r in others:
            ag_copy(r).wait_send()

    def block_wait(which, k):
        @pl.when((lax.rem(k, 2) != core) | (k == me))
        def _():
            pltpu.make_async_copy(blocks[which].at[k], blocks[which].at[k], mat.at[which, k]).wait()

    def split_diag(k):
        block_wait(0, k)
        high, low = split2(dbuf[k])
        dsplit[k, 0:cols, :] = high
        dsplit[k, cols : 2 * cols, :] = low

    def split_coup(k):
        block_wait(1, k)
        high, low = split2(cbuf[k])
        csplit[k, :, 0:cols] = high
        csplit[k, :, cols : 2 * cols] = low

    def narrow(value, weights, dims):
        wide = lax.dot_general(stacked_rows(value), weights, dims, preferred_element_type=F32)
        return (wide[:rows, :cols] + wide[:rows, cols:]) + (wide[rows:, :cols] + wide[rows:, cols:])

    def spread(value, weights, dims):
        both = stacked_rows(value)
        both = jnp.concatenate([both, both], axis=1)
        wide = lax.dot_general(both, weights, dims, preferred_element_type=F32)
        return wide[:rows] + wide[rows:]

    rhs_wait(0)
    gather_start(rpiece[0] + outer[0, at_group(me), :])
    relay_farthest(0, 0)
    relay_farthest(1, 1)
    relay_farthest(0, 1)
    split_diag(0)

    def forward(k, carry):
        pl.when(k > 0)(reduce_sent)
        split_coup(k + 1)
        gather_end()
        solved = narrow(full[...], dsplit[k], nt)
        part[...] = -spread(solved, csplit[k + 1], nt)
        reduce_start()
        ybuf[k] = solved
        gather_sent()
        rhs_wait(k + 1)
        relay_farthest(1, k + 2)
        relay_farthest(0, k + 2)
        split_diag(k + 1)
        gather_start(reduce_end(part[:, at_band(band)] + (rpiece[k + 1] + outer[k + 1, at_group(me), :])))
        return carry

    lax.fori_loop(0, nc - 1, forward, 0)
    reduce_sent()
    gather_end()
    ybuf[nc - 1] = narrow(full[...], dsplit[nc - 1], nt)

    def out_copy(k, source):
        return remote(xbuf.at[k], out_ref.at[at_group(source), :], out_send.at[k], out_recv.at[source], k, band)

    def backward(step, coupled):
        k = nc - 1 - step
        part[...] = spread(ybuf[k] - coupled, dsplit[k], nn)
        reduce_start()
        gather_sent()
        total = reduce_end(part[:, at_band(band)])
        gather_start(total)
        reduce_sent()
        xbuf[k] = total

        @pl.when(k != me)
        def _():
            out_copy(k, me).start()

        @pl.when(k == me)
        def _():
            out_ref[at_group(me), :] = total

        gather_end()
        return narrow(full[...], csplit[k], nn)

    coupled = lax.fori_loop(0, nc - 1, backward, jnp.zeros((rows, cols), F32))
    part[...] = spread(ybuf[0] - coupled, dsplit[0], nn)
    reduce_start()
    gather_sent()
    total = reduce_end(part[:, at_band(band)])
    xbuf[0] = total
    pl.when(me != 0)(lambda: out_copy(0, me).start())

    @pl.when(me == 0)
    def _():
        out_ref[at_group(0), :] = total

    for r in range(1, nc):
        other = lax.rem(me + r, nc)
        out_copy(other, me).wait_send()
        out_copy(me, other).wait_recv()
        rhs_copy(other, me).wait_send()
        slope_chain_copy(other, me).wait_send()
        mode_chain_copy(other, me).wait_send()
        element_copy(other, me).wait_send()
    reduce_sent()
    for r in range(1, nb):
        slope_band_copy(r).wait_send()
        mode_band_copy(r).wait_send()
        band_copy(band_to(r), band).wait_send()

    def sent(which):
        for i in range(3):
            own_copy(which, i).wait_send()

    for which in range(2):
        each_block(which, functools.partial(sent, which))
        for by in (1, 2, 3):

            def relayed(which=which, by=by):
                relay_on(which, by).wait_send()
                if by != 2:
                    pl.when(forwards(by))(lambda: relay_further(which, by).wait_send())

            each_relayed(which, by, relayed)


def on_device(nc, nb, diag_inverse, coupling, elem_stiff, elem_mass, elem_dofs, elem_slab, elem_var, mode, mass_mode, eigenvalue):
    band = lax.axis_index("band")
    cols, width = diag_inverse.shape
    ed, count = elem_dofs.shape
    cap = count // 4
    rows = VARS // nc
    padded = 256
    vmem = pl.BlockSpec(memory_space=pltpu.VMEM)
    anywhere = pl.BlockSpec(memory_space=pl.ANY)
    own_mass = lax.dynamic_slice_in_dim(mass_mode, band * cols, cols)[None, :]
    dma = pltpu.SemaphoreType.DMA
    eigvec_slope, eigval_slope = pl.pallas_call(
        functools.partial(solve_kernel, nc, nb),
        out_shape=(jax.ShapeDtypeStruct((VARS, cols), F32), jax.ShapeDtypeStruct((1, VARS), F32)),
        in_specs=[pl.BlockSpec(memory_space=pltpu.SMEM)] + [anywhere] * 9,
        out_specs=(vmem, vmem),
        scratch_shapes=[
            pltpu.VMEM((ed, count), jnp.int32),
            pltpu.VMEM((1, count), jnp.int32),
            pltpu.VMEM((1, count), jnp.int32),
            pltpu.VMEM((1, cols), F32),
            pltpu.VMEM((1, cols), F32),
            pltpu.VMEM((ed, ed, count), F32),
            pltpu.VMEM((ed, ed, count), F32),
            pltpu.VMEM((8, cols), F32),
            pltpu.VMEM((nc, 8, cols), F32),
            pltpu.VMEM((nc, cols), F32),
            pltpu.VMEM((nc * nb, cols), F32),
            pltpu.VMEM((ed, count), F32),
            pltpu.VMEM((ed, count), F32),
            pltpu.VMEM((nc, 2 * ed + 8, cap), F32),
            pltpu.VMEM((nc, 2 * ed + 8, cap), F32),
            pltpu.VMEM((8, padded), F32),
            pltpu.VMEM((nc, cols, width), F32),
            pltpu.VMEM((nc, width, cols), F32),
            pltpu.VMEM((nc, 2 * cols, width), BF16),
            pltpu.VMEM((nc, width, 2 * cols), BF16),
            pltpu.VMEM((256, 2 * nc * cap), BF16),
            pltpu.VMEM((VARS, width), F32),
            pltpu.VMEM((nb, VARS, cols), F32),
            pltpu.VMEM((VARS, cols), F32),
            pltpu.VMEM((nc, rows, cols), F32),
            pltpu.VMEM((nc, 8, padded), F32),
            pltpu.VMEM((nb, 8, padded), F32),
            pltpu.VMEM((nc, padded, cols), F32),
            pltpu.VMEM((rows, width), F32),
            pltpu.VMEM((nb, rows, cols), F32),
            pltpu.VMEM((rows, cols), F32),
            pltpu.VMEM((rows, width), F32),
            pltpu.VMEM((nc, rows, cols), F32),
            pltpu.VMEM((nc, rows, cols), F32),
            dma((7,)), dma((nc,)), dma((nc,)), dma((nb,)), dma((nb,)), dma((nc,)), dma((nc,)),
            dma((2, nc)), dma((2, 3)), dma((2, 4, 2)),
            dma((nc,)), dma((nc,)), dma((nb,)), dma((nb,)), dma((nc,)), dma((nc,)),
            dma((nb,)), dma((nb,)),
            dma((nb,)), dma((nb,)), dma((nb,)), dma((nb,)), dma((nc,)), dma((nc,)),
        ],
        compiler_params=pltpu.CompilerParams(collective_id=0, has_side_effects=True, vmem_limit_bytes=52 * 1024 * 1024),
        cost_estimate=pl.CostEstimate(flops=10**10, bytes_accessed=10**8, transcendentals=0),
        name="solve",
    )(eigenvalue, diag_inverse, coupling, elem_stiff, elem_mass, elem_dofs, elem_slab.reshape(1, count),
      elem_var.reshape(1, count), mode[None, :], own_mass)
    return eigvec_slope, eigval_slope.reshape(VARS)


def solution(mesh):
    nc, nb = mesh.shape["chain"], mesh.shape["band"]
    in_specs = (
        P(("chain", "band"), None),
        P("chain", "band"),
        P(None, None, ("chain", "band")),
        P(None, None, ("chain", "band")),
        P(None, ("chain", "band")),
        P(("chain", "band"), None),
        P(("chain", "band")),
        P(("chain", "band")),
        P("chain"),
        P(),
    )
    out_specs = (P(None, ("chain", "band")), P())
    return jax.shard_map(functools.partial(on_device, nc, nb), mesh=mesh, in_specs=in_specs, out_specs=out_specs, check_vma=False)
```

```python
import functools
import math

import jax
import jax.numpy as jnp
from jax import lax
from jax.experimental import pallas as pl
from jax.experimental.pallas import tpu as pltpu
from jax.sharding import PartitionSpec as P

MESH = pl.DeviceIdType.MESH
F32 = jnp.float32
BF16 = jnp.bfloat16
VARS = 192


def split2(x):
    high = x.astype(BF16)
    return high, (x - high.astype(F32)).astype(BF16)


def stacked_rows(x):
    high = x.astype(BF16).astype(F32)
    return jnp.concatenate([high, x - high], axis=0).astype(BF16)


def three_way(x):
    high = x.astype(BF16).astype(F32)
    middle = (x - high).astype(BF16).astype(F32)
    return high, middle, x - high - middle


def element_loads(nc, lam_ref, table_ref, stiff_ref, mass_ref, dofs_ref, slab_ref, var_ref,
                  send_ref, slope_ref, mode_at, loads, matrices_here):
    ed, count = dofs_ref.shape
    lanes = table_ref.shape[1]
    cap = send_ref.shape[2]
    lam = lam_ref[0]
    dofs, slab, var = dofs_ref[...], slab_ref[...], var_ref[...]
    row_of = lax.shift_right_logical(dofs, 7) * nc + slab
    lane_of = jnp.bitwise_and(dofs, lanes - 1)
    chunks = count // lanes

    def look(step, found):
        found = list(found)
        for inner in range(8):
            r = step * 8 + inner
            row = jnp.broadcast_to(table_ref[pl.ds(r, 1), :], (ed, lanes))
            for c in range(chunks):
                at = slice(c * lanes, (c + 1) * lanes)
                taken = jnp.take_along_axis(row, lane_of[:, at], axis=1, mode="promise_in_bounds")
                found[c] = jnp.where(row_of[:, at] == r, taken, found[c])
        return tuple(found)

    found = lax.fori_loop(0, table_ref.shape[0] // 8, look, (jnp.zeros((ed, lanes), F32),) * chunks)
    for c in range(chunks):
        mode_at[:, c * lanes : (c + 1) * lanes] = found[c]
    modes = mode_at[...]
    matrices_here()
    for i in range(ed):
        operator = stiff_ref[i] - lam * mass_ref[i]
        loads[i : i + 1, :] = -jnp.sum(operator * modes, axis=0, keepdims=True)
    values = loads[...]
    quadratic = -jnp.sum(modes * values, axis=0, keepdims=True)
    padded = slope_ref.shape[1]
    matches = (lax.broadcasted_iota(jnp.int32, (padded, count), 0) == var).astype(F32).astype(BF16)
    terms = jnp.concatenate(list(three_way(quadratic)) + [jnp.zeros((5, count), F32)], axis=0).astype(BF16)
    nt = (((1,), (1,)), ((), ()))
    sums = lax.dot_general(terms, matches, nt, preferred_element_type=F32)
    slope_ref[...] = jnp.broadcast_to(jnp.sum(sums, axis=0, keepdims=True), slope_ref.shape)
    merged = jnp.zeros((ed, count), F32)
    for i in range(ed):
        merged = merged + jnp.where(dofs == dofs[i : i + 1, :], values[i : i + 1, :], 0.0)
    onehot = (lax.broadcasted_iota(jnp.int32, (nc, count), 0) == slab).astype(F32)
    earlier = lax.broadcasted_iota(jnp.int32, (count, count), 0) < lax.broadcasted_iota(jnp.int32, (count, count), 1)
    rank_all = jnp.dot(onehot.astype(BF16), earlier.astype(F32).astype(BF16), preferred_element_type=F32)
    rank = jnp.sum(onehot * rank_all, axis=0, keepdims=True).astype(jnp.int32)
    slot = slab * cap + rank
    high, middle, low = three_way(merged)
    coarse = lax.shift_right_logical(dofs, 4).astype(F32)
    fine = jnp.bitwise_and(dofs, 15).astype(F32)
    var_rows = jnp.concatenate([var.astype(F32), jnp.zeros((7, count), F32)], axis=0)
    data = jnp.concatenate([high, middle, low, coarse, fine, var_rows], axis=0).astype(BF16)
    for k in range(nc):
        place = (lax.broadcasted_iota(jnp.int32, (cap, count), 0) + k * cap == slot).astype(F32).astype(BF16)
        packed = lax.dot_general(data, place, nt, preferred_element_type=F32)
        send_ref[k, 0:ed, :] = (packed[0:ed] + packed[ed : 2 * ed]) + packed[2 * ed : 3 * ed]
        send_ref[k, ed : 2 * ed, :] = packed[3 * ed : 4 * ed] * 16.0 + packed[4 * ed : 5 * ed]
        send_ref[k, 2 * ed : 2 * ed + 8, :] = packed[5 * ed : 5 * ed + 8]


def solve_kernel(nc, nb, lam_ref, diag_ref, coup_ref, stiff_ref, emass_ref, dofs_in, slab_in, var_in, mode_in, mass_in,
                 out_ref, slope_out, dofs_ref, slab_ref, var_ref, mode_ref, mass_ref, stiff, emass, mode_tile, mode_chain, mode_group, table, mode_at, loads, send_ref, got_ref, slope_ref,
                 dbuf, cbuf, dsplit, csplit, spread_ref, rpart, rslots, rsum, rpiece, sl_chain, sl_band, outer,
                 part, slots, piece, full, ybuf, xbuf,
                 el_sem, mc_send, mc_recv, mb_send, mb_recv, ex_send, ex_recv, mat, own_send, relay_send, slc_send, slc_recv, slb_send, slb_recv, r_send, r_recv, rq_send, rq_recv,
                 rs_send, rs_recv, ag_send, ag_recv, out_send, out_recv):
    me, band = lax.axis_index("chain"), lax.axis_index("band")
    x_len = nc // 2
    my_x, core = me // 2, lax.rem(me, 2)
    rows, width = part.shape
    cols = width // nb
    nvars = rpart.shape[0]
    sibling = 2 * my_x + 1 - core
    blocks = (dbuf, cbuf)
    nt = (((1,), (1,)), ((), ()))
    nn = (((1,), (0,)), ((), ()))

    def at_band(b):
        return pl.ds(pl.multiple_of(b * cols, cols), cols)

    side = math.isqrt(nb)
    hops = lambda r: min(r // side, side - r // side) + min(r % side, side - r % side)
    others = sorted(range(1, nb), key=lambda r: (-hops(r), (r * 7) % 16))
    band_z, band_y = band // side, lax.rem(band, side)

    def band_to(r):
        return lax.rem(band_z + r // side, side) * side + lax.rem(band_y + r % side, side)

    def band_from(r):
        return lax.rem(band_z + side - r // side, side) * side + lax.rem(band_y + side - r % side, side)

    def at_group(c):
        return pl.ds(pl.multiple_of(c * rows, 8), rows)

    def along_x(by):
        return 2 * lax.rem(my_x + by + x_len, x_len) + core

    def remote(src, dst, send, recv, chain, to_band):
        return pltpu.make_async_remote_copy(src_ref=src, dst_ref=dst, send_sem=send, recv_sem=recv,
                                            device_id=(chain, to_band), device_id_type=MESH)

    def each_block(which, work):
        if which == 0:
            work()
        else:
            pl.when(me != 0)(work)

    def own_load(which):
        return pltpu.make_async_copy((diag_ref, coup_ref)[which], blocks[which].at[me], mat.at[which, me])

    def own_copy(which, i):
        to = (along_x(1), along_x(-1), sibling)[i]
        return remote((diag_ref, coup_ref)[which], blocks[which].at[me], own_send.at[which, i], mat.at[which, me], to, band)

    small = ((mode_in, mode_ref), (mass_in, mass_ref), (dofs_in, dofs_ref), (slab_in, slab_ref), (var_in, var_ref))
    small_loads = [pltpu.make_async_copy(src, dst, el_sem.at[2 + i]) for i, (src, dst) in enumerate(small)]
    for load in small_loads:
        load.start()
    stiff_load = pltpu.make_async_copy(stiff_ref, stiff, el_sem.at[0])
    emass_load = pltpu.make_async_copy(emass_ref, emass, el_sem.at[1])
    stiff_load.start()
    emass_load.start()
    for which in range(2):
        each_block(which, lambda which=which: own_load(which).start())
    for load in small_loads:
        load.wait()
    line = lax.broadcasted_iota(jnp.int32, mode_tile.shape, 0)
    mode_tile[...] = jnp.where(line == 0, mode_ref[...], jnp.where(line == 1, mass_ref[...], 0.0))

    barrier = pltpu.get_barrier_semaphore()
    for r in range(1, nb):
        pl.semaphore_signal(barrier, inc=1, device_id=(me, band_to(r)), device_id_type=MESH)
    for r in range(1, nc):
        pl.semaphore_signal(barrier, inc=1, device_id=(lax.rem(me + r, nc), band), device_id_type=MESH)
    pl.semaphore_wait(barrier, nb + nc - 2)

    def send_own(which):
        for i in range(3):
            own_copy(which, i).start()

    def relay_on(which, by):
        slab = along_x(-by)
        block = blocks[which].at[slab]
        return remote(block, block, relay_send.at[which, by, 0], mat.at[which, slab], sibling, band)

    def relay_further(which, by):
        slab = along_x(-by)
        block = blocks[which].at[slab]
        return remote(block, block, relay_send.at[which, by, 1], mat.at[which, slab], along_x(1 if by == 1 else -1), band)

    def each_relayed(which, by, work):
        if which == 0:
            work()
        else:
            pl.when(along_x(-by) != 0)(work)

    def forwards(by):
        return {1: core == 0, 3: core == 1}[by]

    def relay(which, by):
        slab = along_x(-by)

        def work():
            pltpu.make_async_copy(blocks[which].at[slab], blocks[which].at[slab], mat.at[which, slab]).wait()
            if by != 2:
                pl.when(forwards(by))(lambda: relay_further(which, by).start())
            relay_on(which, by).start()

        each_relayed(which, by, work)

    def relay_farthest(which, k):
        pl.when(k == along_x(2))(lambda: relay(which, 2))

    def first_sends():
        pl.when(me != 1)(lambda: send_own(0))
        pl.when(me == 1)(lambda: send_own(1))

    def second_sends():
        pl.when(me == 1)(lambda: send_own(0))
        pl.when((me != 0) & (me != 1))(lambda: send_own(1))

    def first_relays():
        pl.when(core == 0)(lambda: relay(0, 1))

        @pl.when(core == 1)
        def _():
            pl.when(along_x(1) != 1)(lambda: relay(0, 3))
            pl.when(along_x(1) == 1)(lambda: relay(1, 3))

    def second_relays():
        @pl.when(core == 0)
        def _():
            relay(1, 1)
            relay(0, 3)
            relay(1, 3)

        @pl.when(core == 1)
        def _():
            pl.when(along_x(1) != 1)(lambda: relay(1, 3))
            pl.when(along_x(1) == 1)(lambda: relay(0, 3))
            relay(0, 1)
            relay(1, 1)

    def mode_chain_copy(to, source):
        return remote(mode_tile, mode_chain.at[source], mc_send.at[to], mc_recv.at[source], to, band)

    for r in range(1, nc):
        mode_chain_copy(lax.rem(me + r, nc), me).start()
    mode_chain[me] = mode_tile[...]

    first_sends()
    for r in range(1, nc):
        mode_chain_copy(me, lax.rem(me + r, nc)).wait_recv()
    line = lax.broadcasted_iota(jnp.int32, (nc, cols), 0)
    whole = jnp.zeros((nc, cols), F32)
    for c in range(nc):
        whole = jnp.where(line == c, mode_chain[c, 0:1, :], whole)
    mode_group[...] = whole

    def at_rows(b):
        return table.at[pl.ds(pl.multiple_of(b * nc, 8), nc), :]

    def mode_band_copy(r):
        to = band_to(r)
        return remote(mode_group, at_rows(band), mb_send.at[r], mb_recv.at[r], me, to)

    def mode_band_arrival(r):
        source = band_from(r)
        return remote(mode_group, at_rows(source), mb_send.at[r], mb_recv.at[r], me, source)

    for r in others:
        mode_band_copy(r).start()
    table[pl.ds(pl.multiple_of(band * nc, 8), nc), :] = whole
    for r in range(1, nb):
        mode_band_arrival(r).wait_recv()

    def matrices_here():
        stiff_load.wait()
        emass_load.wait()

    element_loads(nc, lam_ref, table, stiff, emass, dofs_ref, slab_ref, var_ref, send_ref, slope_ref, mode_at, loads, matrices_here)

    def element_copy(to, source):
        return remote(send_ref.at[to], got_ref.at[source], ex_send.at[to], ex_recv.at[source], to, band)

    def slope_chain_copy(to, source):
        return remote(slope_ref, sl_chain.at[source], slc_send.at[to], slc_recv.at[source], to, band)

    for r in range(1, nc):
        element_copy(lax.rem(me + r, nc), me).start()
        slope_chain_copy(lax.rem(me + r, nc), me).start()
    sl_chain[me] = slope_ref[...]
    got_ref[me] = send_ref[me]
    first_relays()
    second_sends()
    for r in range(1, nc):
        element_copy(me, lax.rem(me + r, nc)).wait_recv()

    for r in range(1, nc):
        slope_chain_copy(me, lax.rem(me + r, nc)).wait_recv()
    total = sl_chain[0]
    for c in range(1, nc):
        total = total + sl_chain[c]

    def slope_band_copy(r):
        to = band_to(r)
        return remote(sl_band.at[band], sl_band.at[band], slb_send.at[r], slb_recv.at[r], me, to)

    def slope_band_arrival(r):
        source = band_from(r)
        return remote(sl_band.at[source], sl_band.at[source], slb_send.at[r], slb_recv.at[r], me, source)

    sl_band[band] = total
    for r in others:
        slope_band_copy(r).start()

    def slope_term():
        for r in others:
            slope_band_arrival(r).wait_recv()
        total = sl_band[0]
        for b in range(1, nb):
            total = total + sl_band[b]
        slope_out[...] = total[0:1, :nvars]
        line = lax.broadcasted_iota(jnp.int32, total.shape, 0)
        high, middle, low = three_way(total)
        slope_terms = jnp.where((line == 0) | (line == 3) | (line == 5), high, 0.0)
        slope_terms = jnp.where((line == 1) | (line == 4), middle, jnp.where(line == 2, low, slope_terms))
        line = lax.broadcasted_iota(jnp.int32, (8, cols), 0)
        for k in range(nc):
            high, middle, low = three_way(jnp.broadcast_to(mode_chain[k, 1:2, :], (8, cols)))
            mass_terms = jnp.where(line < 3, high, jnp.where(line < 5, middle, jnp.where(line == 5, low, 0.0)))
            outer[k] = lax.dot_general(slope_terms.astype(BF16), mass_terms.astype(BF16), (((0,), (0,)), ((), ())), preferred_element_type=F32)

    cap = got_ref.shape[2]
    ed = (got_ref.shape[1] - 8) // 2
    block = spread_ref.shape[0]
    lines = 256
    base = lax.broadcasted_iota(jnp.int32, (lines, cap), 0).astype(F32).astype(BF16)
    variable = lax.broadcasted_iota(jnp.int32, (nvars, cap), 0)
    matches = [(variable == got_ref[s, 2 * ed : 2 * ed + 1, :].astype(jnp.int32)).astype(F32).astype(BF16) for s in range(nc)]
    matches = jnp.concatenate(matches + matches, axis=1)

    def band_copy(to, source):
        return remote(rpart.at[:, at_band(to)], rslots.at[source], rq_send.at[to], rq_recv.at[source], me, to)

    per_block = block // cols

    def one_block(step, carry):
        n = lax.rem(step + 1 + band // per_block, width // block)

        def one_source(s, inner):
            values = got_ref[s, 0:ed, :]
            high = values.astype(BF16)
            low = (values - high.astype(F32)).astype(BF16)
            dofs = got_ref[s, ed : 2 * ed, :].astype(jnp.int32) - n * block
            for part_no in range(block // lines):
                shifted = dofs - part_no * lines
                shifted = jnp.where((shifted >= 0) & (shifted < lines), shifted, -1)
                place = shifted.astype(F32).astype(BF16)
                total_high = jnp.zeros((lines, cap), BF16)
                total_low = jnp.zeros((lines, cap), BF16)
                for i in range(ed):
                    hit = base == place[i : i + 1, :]
                    total_high = jnp.where(hit, high[i : i + 1, :], total_high)
                    total_low = jnp.where(hit, low[i : i + 1, :], total_low)
                at = pl.ds(pl.multiple_of(s * cap, cap), cap)
                spread_ref[part_no * lines : (part_no + 1) * lines, at] = total_high
                at = pl.ds(pl.multiple_of((s + nc) * cap, cap), cap)
                spread_ref[part_no * lines : (part_no + 1) * lines, at] = total_low
            return inner

        lax.fori_loop(0, nc, one_source, 0)
        at = pl.ds(pl.multiple_of(n * block, block), block)
        rpart[:, at] = lax.dot_general(matches, spread_ref[...], nt, preferred_element_type=F32)

        for j in range(per_block):
            to = n * per_block + j
            pl.when(to != band)(lambda to=to: band_copy(to, band).start())

        return carry

    lax.fori_loop(0, width // block, one_block, 0)

    slope_term()
    total = rpart[:, at_band(band)]
    for r in others:
        band_copy(band, band_from(r)).wait_recv()
        total = total + rslots[band_from(r)]
    rsum[...] = total

    def rhs_copy(to, source):
        return remote(rsum.at[at_group(to), :], rpiece.at[source], r_send.at[to], r_recv.at[source], to, band)

    for r in range(1, nc):
        rhs_copy(lax.rem(me + r, nc), me).start()
    rpiece[me] = rsum[at_group(me), :]

    def rhs_wait(k):
        pl.when(k != me)(lambda: rhs_copy(me, k).wait_recv())

    second_relays()

    def rs_copy(r):
        to = band_to(r)
        return remote(part.at[:, at_band(to)], slots.at[r], rs_send.at[r], rs_recv.at[r], me, to)

    def ag_copy(r):
        to = band_to(r)
        return remote(piece, full.at[:, at_band(band)], ag_send.at[r], ag_recv.at[r], me, to)

    def ag_arrival(r):
        source = band_from(r)
        return remote(piece, full.at[:, at_band(source)], ag_send.at[r], ag_recv.at[r], me, source)

    def reduce_start():
        for r in others:
            rs_copy(r).start()

    def reduce_end(own):
        total = own
        for r in reversed(others):
            rs_copy(r).wait_recv()
            total = total + slots[r]
        return total

    def reduce_sent():
        for r in others:
            rs_copy(r).wait_send()

    def gather_start(value):
        piece[...] = value
        for r in others:
            ag_copy(r).start()
        full[:, at_band(band)] = value

    def gather_end():
        for r in reversed(others):
            ag_arrival(r).wait_recv()

    def gather_sent():
        for r in others:
            ag_copy(r).wait_send()

    def block_wait(which, k):
        @pl.when((lax.rem(k, 2) != core) | (k == me))
        def _():
            pltpu.make_async_copy(blocks[which].at[k], blocks[which].at[k], mat.at[which, k]).wait()

    def split_diag(k):
        block_wait(0, k)
        high, low = split2(dbuf[k])
        dsplit[k, 0:cols, :] = high
        dsplit[k, cols : 2 * cols, :] = low

    def split_coup(k):
        block_wait(1, k)
        high, low = split2(cbuf[k])
        csplit[k, :, 0:cols] = high
        csplit[k, :, cols : 2 * cols] = low

    def narrow(value, weights, dims):
        wide = lax.dot_general(stacked_rows(value), weights, dims, preferred_element_type=F32)
        return (wide[:rows, :cols] + wide[:rows, cols:]) + (wide[rows:, :cols] + wide[rows:, cols:])

    def spread(value, weights, dims):
        both = stacked_rows(value)
        both = jnp.concatenate([both, both], axis=1)
        wide = lax.dot_general(both, weights, dims, preferred_element_type=F32)
        return wide[:rows] + wide[rows:]

    rhs_wait(0)
    gather_start(rpiece[0] + outer[0, at_group(me), :])
    relay_farthest(0, 0)
    relay_farthest(1, 1)
    relay_farthest(0, 1)
    split_diag(0)

    def forward(k, carry):
        pl.when(k > 0)(reduce_sent)
        split_coup(k + 1)
        gather_end()
        solved = narrow(full[...], dsplit[k], nt)
        part[...] = -spread(solved, csplit[k + 1], nt)
        reduce_start()
        ybuf[k] = solved
        gather_sent()
        rhs_wait(k + 1)
        relay_farthest(1, k + 2)
        relay_farthest(0, k + 2)
        split_diag(k + 1)
        gather_start(reduce_end(part[:, at_band(band)] + (rpiece[k + 1] + outer[k + 1, at_group(me), :])))
        return carry

    lax.fori_loop(0, nc - 1, forward, 0)
    reduce_sent()
    gather_end()
    ybuf[nc - 1] = narrow(full[...], dsplit[nc - 1], nt)

    def out_copy(k, source):
        return remote(xbuf.at[k], out_ref.at[at_group(source), :], out_send.at[k], out_recv.at[source], k, band)

    def backward(step, coupled):
        k = nc - 1 - step
        part[...] = spread(ybuf[k] - coupled, dsplit[k], nn)
        reduce_start()
        gather_sent()
        total = reduce_end(part[:, at_band(band)])
        gather_start(total)
        reduce_sent()
        xbuf[k] = total

        @pl.when(k != me)
        def _():
            out_copy(k, me).start()

        @pl.when(k == me)
        def _():
            out_ref[at_group(me), :] = total

        gather_end()
        return narrow(full[...], csplit[k], nn)

    coupled = lax.fori_loop(0, nc - 1, backward, jnp.zeros((rows, cols), F32))
    part[...] = spread(ybuf[0] - coupled, dsplit[0], nn)
    reduce_start()
    gather_sent()
    total = reduce_end(part[:, at_band(band)])
    xbuf[0] = total
    pl.when(me != 0)(lambda: out_copy(0, me).start())

    @pl.when(me == 0)
    def _():
        out_ref[at_group(0), :] = total

    for r in range(1, nc):
        other = lax.rem(me + r, nc)
        out_copy(other, me).wait_send()
        out_copy(me, other).wait_recv()
        rhs_copy(other, me).wait_send()
        slope_chain_copy(other, me).wait_send()
        mode_chain_copy(other, me).wait_send()
        element_copy(other, me).wait_send()
    reduce_sent()
    for r in range(1, nb):
        slope_band_copy(r).wait_send()
        mode_band_copy(r).wait_send()
        band_copy(band_to(r), band).wait_send()

    def sent(which):
        for i in range(3):
            own_copy(which, i).wait_send()

    for which in range(2):
        each_block(which, functools.partial(sent, which))
        for by in (1, 2, 3):

            def relayed(which=which, by=by):
                relay_on(which, by).wait_send()
                if by != 2:
                    pl.when(forwards(by))(lambda: relay_further(which, by).wait_send())

            each_relayed(which, by, relayed)


def on_device(nc, nb, diag_inverse, coupling, elem_stiff, elem_mass, elem_dofs, elem_slab, elem_var, mode, mass_mode, eigenvalue):
    band = lax.axis_index("band")
    cols, width = diag_inverse.shape
    ed, count = elem_dofs.shape
    cap = count // 4
    rows = VARS // nc
    padded = 256
    vmem = pl.BlockSpec(memory_space=pltpu.VMEM)
    anywhere = pl.BlockSpec(memory_space=pl.ANY)
    own_mass = lax.dynamic_slice_in_dim(mass_mode, band * cols, cols)[None, :]
    dma = pltpu.SemaphoreType.DMA
    eigvec_slope, eigval_slope = pl.pallas_call(
        functools.partial(solve_kernel, nc, nb),
        out_shape=(jax.ShapeDtypeStruct((VARS, cols), F32), jax.ShapeDtypeStruct((1, VARS), F32)),
        in_specs=[pl.BlockSpec(memory_space=pltpu.SMEM)] + [anywhere] * 9,
        out_specs=(vmem, vmem),
        scratch_shapes=[
            pltpu.VMEM((ed, count), jnp.int32),
            pltpu.VMEM((1, count), jnp.int32),
            pltpu.VMEM((1, count), jnp.int32),
            pltpu.VMEM((1, cols), F32),
            pltpu.VMEM((1, cols), F32),
            pltpu.VMEM((ed, ed, count), F32),
            pltpu.VMEM((ed, ed, count), F32),
            pltpu.VMEM((8, cols), F32),
            pltpu.VMEM((nc, 8, cols), F32),
            pltpu.VMEM((nc, cols), F32),
            pltpu.VMEM((nc * nb, cols), F32),
            pltpu.VMEM((ed, count), F32),
            pltpu.VMEM((ed, count), F32),
            pltpu.VMEM((nc, 2 * ed + 8, cap), F32),
            pltpu.VMEM((nc, 2 * ed + 8, cap), F32),
            pltpu.VMEM((8, padded), F32),
            pltpu.VMEM((nc, cols, width), F32),
            pltpu.VMEM((nc, width, cols), F32),
            pltpu.VMEM((nc, 2 * cols, width), BF16),
            pltpu.VMEM((nc, width, 2 * cols), BF16),
            pltpu.VMEM((256, 2 * nc * cap), BF16),
            pltpu.VMEM((VARS, width), F32),
            pltpu.VMEM((nb, VARS, cols), F32),
            pltpu.VMEM((VARS, cols), F32),
            pltpu.VMEM((nc, rows, cols), F32),
            pltpu.VMEM((nc, 8, padded), F32),
            pltpu.VMEM((nb, 8, padded), F32),
            pltpu.VMEM((nc, padded, cols), F32),
            pltpu.VMEM((rows, width), F32),
            pltpu.VMEM((nb, rows, cols), F32),
            pltpu.VMEM((rows, cols), F32),
            pltpu.VMEM((rows, width), F32),
            pltpu.VMEM((nc, rows, cols), F32),
            pltpu.VMEM((nc, rows, cols), F32),
            dma((7,)), dma((nc,)), dma((nc,)), dma((nb,)), dma((nb,)), dma((nc,)), dma((nc,)),
            dma((2, nc)), dma((2, 3)), dma((2, 4, 2)),
            dma((nc,)), dma((nc,)), dma((nb,)), dma((nb,)), dma((nc,)), dma((nc,)),
            dma((nb,)), dma((nb,)),
            dma((nb,)), dma((nb,)), dma((nb,)), dma((nb,)), dma((nc,)), dma((nc,)),
        ],
        compiler_params=pltpu.CompilerParams(collective_id=0, has_side_effects=True, vmem_limit_bytes=52 * 1024 * 1024),
        cost_estimate=pl.CostEstimate(flops=10**10, bytes_accessed=10**8, transcendentals=0),
        name="solve",
    )(eigenvalue, diag_inverse, coupling, elem_stiff, elem_mass, elem_dofs, elem_slab.reshape(1, count),
      elem_var.reshape(1, count), mode[None, :], own_mass)
    return eigvec_slope, eigval_slope.reshape(VARS)


def solution(mesh):
    nc, nb = mesh.shape["chain"], mesh.shape["band"]
    in_specs = (
        P(("chain", "band"), None),
        P("chain", "band"),
        P(None, None, ("chain", "band")),
        P(None, None, ("chain", "band")),
        P(None, ("chain", "band")),
        P(("chain", "band"), None),
        P(("chain", "band")),
        P(("chain", "band")),
        P("chain"),
        P(),
    )
    out_specs = (P(None, ("chain", "band")), P())
    return jax.shard_map(functools.partial(on_device, nc, nb), mesh=mesh, in_specs=in_specs, out_specs=out_specs, check_vma=False)
```

```python
import functools
import math

import jax
import jax.numpy as jnp
from jax import lax
from jax.experimental import pallas as pl
from jax.experimental.pallas import tpu as pltpu
from jax.sharding import PartitionSpec as P

MESH = pl.DeviceIdType.MESH
F32 = jnp.float32
BF16 = jnp.bfloat16
VARS = 192


def split2(x):
    high = x.astype(BF16)
    return high, (x - high.astype(F32)).astype(BF16)


def stacked_rows(x):
    high = x.astype(BF16).astype(F32)
    return jnp.concatenate([high, x - high], axis=0).astype(BF16)


def three_way(x):
    high = x.astype(BF16).astype(F32)
    middle = (x - high).astype(BF16).astype(F32)
    return high, middle, x - high - middle


def element_loads(nc, lam_ref, table_ref, stiff_ref, mass_ref, dofs_ref, slab_ref, var_ref,
                  send_ref, slope_ref, mode_at, loads, matrices_here):
    ed, count = dofs_ref.shape
    lanes = table_ref.shape[1]
    cap = send_ref.shape[2]
    lam = lam_ref[0]
    dofs, slab, var = dofs_ref[...], slab_ref[...], var_ref[...]
    row_of = lax.shift_right_logical(dofs, 7) * nc + slab
    lane_of = jnp.bitwise_and(dofs, lanes - 1)
    chunks = count // lanes

    def look(step, found):
        found = list(found)
        for inner in range(8):
            r = step * 8 + inner
            row = jnp.broadcast_to(table_ref[pl.ds(r, 1), :], (ed, lanes))
            for c in range(chunks):
                at = slice(c * lanes, (c + 1) * lanes)
                taken = jnp.take_along_axis(row, lane_of[:, at], axis=1, mode="promise_in_bounds")
                found[c] = jnp.where(row_of[:, at] == r, taken, found[c])
        return tuple(found)

    found = lax.fori_loop(0, table_ref.shape[0] // 8, look, (jnp.zeros((ed, lanes), F32),) * chunks)
    for c in range(chunks):
        mode_at[:, c * lanes : (c + 1) * lanes] = found[c]
    modes = mode_at[...]
    matrices_here()
    for i in range(ed):
        operator = stiff_ref[i] - lam * mass_ref[i]
        loads[i : i + 1, :] = -jnp.sum(operator * modes, axis=0, keepdims=True)
    values = loads[...]
    quadratic = -jnp.sum(modes * values, axis=0, keepdims=True)
    padded = slope_ref.shape[1]
    matches = (lax.broadcasted_iota(jnp.int32, (padded, count), 0) == var).astype(F32).astype(BF16)
    terms = jnp.concatenate(list(three_way(quadratic)) + [jnp.zeros((5, count), F32)], axis=0).astype(BF16)
    nt = (((1,), (1,)), ((), ()))
    sums = lax.dot_general(terms, matches, nt, preferred_element_type=F32)
    slope_ref[...] = jnp.broadcast_to(jnp.sum(sums, axis=0, keepdims=True), slope_ref.shape)
    merged = jnp.zeros((ed, count), F32)
    for i in range(ed):
        merged = merged + jnp.where(dofs == dofs[i : i + 1, :], values[i : i + 1, :], 0.0)
    onehot = (lax.broadcasted_iota(jnp.int32, (nc, count), 0) == slab).astype(F32)
    earlier = lax.broadcasted_iota(jnp.int32, (count, count), 0) < lax.broadcasted_iota(jnp.int32, (count, count), 1)
    rank_all = jnp.dot(onehot.astype(BF16), earlier.astype(F32).astype(BF16), preferred_element_type=F32)
    rank = jnp.sum(onehot * rank_all, axis=0, keepdims=True).astype(jnp.int32)
    slot = slab * cap + rank
    high, middle, low = three_way(merged)
    coarse = lax.shift_right_logical(dofs, 4).astype(F32)
    fine = jnp.bitwise_and(dofs, 15).astype(F32)
    var_rows = jnp.concatenate([var.astype(F32), jnp.zeros((7, count), F32)], axis=0)
    data = jnp.concatenate([high, middle, low, coarse, fine, var_rows], axis=0).astype(BF16)
    for k in range(nc):
        place = (lax.broadcasted_iota(jnp.int32, (cap, count), 0) + k * cap == slot).astype(F32).astype(BF16)
        packed = lax.dot_general(data, place, nt, preferred_element_type=F32)
        send_ref[k, 0:ed, :] = (packed[0:ed] + packed[ed : 2 * ed]) + packed[2 * ed : 3 * ed]
        send_ref[k, ed : 2 * ed, :] = packed[3 * ed : 4 * ed] * 16.0 + packed[4 * ed : 5 * ed]
        send_ref[k, 2 * ed : 2 * ed + 8, :] = packed[5 * ed : 5 * ed + 8]


def solve_kernel(nc, nb, lam_ref, diag_ref, coup_ref, stiff_ref, emass_ref, dofs_in, slab_in, var_in, mode_in, mass_in,
                 out_ref, slope_out, dofs_ref, slab_ref, var_ref, mode_ref, mass_ref, stiff, emass, mode_tile, mode_chain, mode_group, table, mode_at, loads, send_ref, got_ref, slope_ref,
                 dbuf, cbuf, dsplit, csplit, spread_ref, rpart, rslots, rsum, rpiece, sl_chain, sl_band, outer,
                 part, slots, piece, full, ybuf, xbuf,
                 el_sem, mc_send, mc_recv, mb_send, mb_recv, ex_send, ex_recv, mat, own_send, relay_send, slc_send, slc_recv, slb_send, slb_recv, r_send, r_recv, rq_send, rq_recv,
                 rs_send, rs_recv, ag_send, ag_recv, out_send, out_recv):
    me, band = lax.axis_index("chain"), lax.axis_index("band")
    x_len = nc // 2
    my_x, core = me // 2, lax.rem(me, 2)
    rows, width = part.shape
    cols = width // nb
    nvars = rpart.shape[0]
    sibling = 2 * my_x + 1 - core
    blocks = (dbuf, cbuf)
    nt = (((1,), (1,)), ((), ()))
    nn = (((1,), (0,)), ((), ()))

    def at_band(b):
        return pl.ds(pl.multiple_of(b * cols, cols), cols)

    side = math.isqrt(nb)
    hops = lambda r: min(r // side, side - r // side) + min(r % side, side - r % side)
    others = sorted(range(1, nb), key=lambda r: (-hops(r), (r * 7) % 16))
    band_z, band_y = band // side, lax.rem(band, side)

    towards = {r: lax.rem(band_z + r // side, side) * side + lax.rem(band_y + r % side, side) for r in others}
    behind = {r: lax.rem(band_z + side - r // side, side) * side + lax.rem(band_y + side - r % side, side) for r in others}
    band_to, band_from = towards.__getitem__, behind.__getitem__

    def at_group(c):
        return pl.ds(pl.multiple_of(c * rows, 8), rows)

    def along_x(by):
        return 2 * lax.rem(my_x + by + x_len, x_len) + core

    def remote(src, dst, send, recv, chain, to_band):
        return pltpu.make_async_remote_copy(src_ref=src, dst_ref=dst, send_sem=send, recv_sem=recv,
                                            device_id=(chain, to_band), device_id_type=MESH)

    def each_block(which, work):
        if which == 0:
            work()
        else:
            pl.when(me != 0)(work)

    def own_load(which):
        return pltpu.make_async_copy((diag_ref, coup_ref)[which], blocks[which].at[me], mat.at[which, me])

    def own_copy(which, i):
        to = (along_x(1), along_x(-1), sibling)[i]
        return remote((diag_ref, coup_ref)[which], blocks[which].at[me], own_send.at[which, i], mat.at[which, me], to, band)

    small = ((mode_in, mode_ref), (mass_in, mass_ref), (dofs_in, dofs_ref), (slab_in, slab_ref), (var_in, var_ref))
    small_loads = [pltpu.make_async_copy(src, dst, el_sem.at[2 + i]) for i, (src, dst) in enumerate(small)]
    for load in small_loads:
        load.start()
    stiff_load = pltpu.make_async_copy(stiff_ref, stiff, el_sem.at[0])
    emass_load = pltpu.make_async_copy(emass_ref, emass, el_sem.at[1])
    stiff_load.start()
    emass_load.start()
    for which in range(2):
        each_block(which, lambda which=which: own_load(which).start())
    for load in small_loads:
        load.wait()
    line = lax.broadcasted_iota(jnp.int32, mode_tile.shape, 0)
    mode_tile[...] = jnp.where(line == 0, mode_ref[...], jnp.where(line == 1, mass_ref[...], 0.0))

    barrier = pltpu.get_barrier_semaphore()
    for r in range(1, nb):
        pl.semaphore_signal(barrier, inc=1, device_id=(me, band_to(r)), device_id_type=MESH)
    for r in range(1, nc):
        pl.semaphore_signal(barrier, inc=1, device_id=(lax.rem(me + r, nc), band), device_id_type=MESH)
    pl.semaphore_wait(barrier, nb + nc - 2)

    def send_own(which):
        for i in range(3):
            own_copy(which, i).start()

    def relay_on(which, by):
        slab = along_x(-by)
        block = blocks[which].at[slab]
        return remote(block, block, relay_send.at[which, by, 0], mat.at[which, slab], sibling, band)

    def relay_further(which, by):
        slab = along_x(-by)
        block = blocks[which].at[slab]
        return remote(block, block, relay_send.at[which, by, 1], mat.at[which, slab], along_x(1 if by == 1 else -1), band)

    def each_relayed(which, by, work):
        if which == 0:
            work()
        else:
            pl.when(along_x(-by) != 0)(work)

    def forwards(by):
        return {1: core == 0, 3: core == 1}[by]

    def relay(which, by):
        slab = along_x(-by)

        def work():
            pltpu.make_async_copy(blocks[which].at[slab], blocks[which].at[slab], mat.at[which, slab]).wait()
            if by != 2:
                pl.when(forwards(by))(lambda: relay_further(which, by).start())
            relay_on(which, by).start()

        each_relayed(which, by, work)

    def relay_farthest(which, k):
        pl.when(k == along_x(2))(lambda: relay(which, 2))

    def first_sends():
        pl.when(me != 1)(lambda: send_own(0))
        pl.when(me == 1)(lambda: send_own(1))

    def second_sends():
        pl.when(me == 1)(lambda: send_own(0))
        pl.when((me != 0) & (me != 1))(lambda: send_own(1))

    def first_relays():
        pl.when(core == 0)(lambda: relay(0, 1))

        @pl.when(core == 1)
        def _():
            pl.when(along_x(1) != 1)(lambda: relay(0, 3))
            pl.when(along_x(1) == 1)(lambda: relay(1, 3))

    def second_relays():
        @pl.when(core == 0)
        def _():
            relay(1, 1)
            relay(0, 3)
            relay(1, 3)

        @pl.when(core == 1)
        def _():
            pl.when(along_x(1) != 1)(lambda: relay(1, 3))
            pl.when(along_x(1) == 1)(lambda: relay(0, 3))
            relay(0, 1)
            relay(1, 1)

    def mode_chain_copy(to, source):
        return remote(mode_tile, mode_chain.at[source], mc_send.at[to], mc_recv.at[source], to, band)

    for r in range(1, nc):
        mode_chain_copy(lax.rem(me + r, nc), me).start()
    mode_chain[me] = mode_tile[...]

    first_sends()
    for r in range(1, nc):
        mode_chain_copy(me, lax.rem(me + r, nc)).wait_recv()
    line = lax.broadcasted_iota(jnp.int32, (nc, cols), 0)
    whole = jnp.zeros((nc, cols), F32)
    for c in range(nc):
        whole = jnp.where(line == c, mode_chain[c, 0:1, :], whole)
    mode_group[...] = whole

    def at_rows(b):
        return table.at[pl.ds(pl.multiple_of(b * nc, 8), nc), :]

    def mode_band_copy(r):
        to = band_to(r)
        return remote(mode_group, at_rows(band), mb_send.at[r], mb_recv.at[r], me, to)

    def mode_band_arrival(r):
        source = band_from(r)
        return remote(mode_group, at_rows(source), mb_send.at[r], mb_recv.at[r], me, source)

    for r in others:
        mode_band_copy(r).start()
    table[pl.ds(pl.multiple_of(band * nc, 8), nc), :] = whole
    for r in range(1, nb):
        mode_band_arrival(r).wait_recv()

    def matrices_here():
        stiff_load.wait()
        emass_load.wait()

    element_loads(nc, lam_ref, table, stiff, emass, dofs_ref, slab_ref, var_ref, send_ref, slope_ref, mode_at, loads, matrices_here)

    def element_copy(to, source):
        return remote(send_ref.at[to], got_ref.at[source], ex_send.at[to], ex_recv.at[source], to, band)

    def slope_chain_copy(to, source):
        return remote(slope_ref, sl_chain.at[source], slc_send.at[to], slc_recv.at[source], to, band)

    for r in range(1, nc):
        element_copy(lax.rem(me + r, nc), me).start()
        slope_chain_copy(lax.rem(me + r, nc), me).start()
    sl_chain[me] = slope_ref[...]
    got_ref[me] = send_ref[me]
    first_relays()
    second_sends()
    for r in range(1, nc):
        element_copy(me, lax.rem(me + r, nc)).wait_recv()

    for r in range(1, nc):
        slope_chain_copy(me, lax.rem(me + r, nc)).wait_recv()
    total = sl_chain[0]
    for c in range(1, nc):
        total = total + sl_chain[c]

    def slope_band_copy(r):
        to = band_to(r)
        return remote(sl_band.at[band], sl_band.at[band], slb_send.at[r], slb_recv.at[r], me, to)

    def slope_band_arrival(r):
        source = band_from(r)
        return remote(sl_band.at[source], sl_band.at[source], slb_send.at[r], slb_recv.at[r], me, source)

    sl_band[band] = total
    for r in others:
        slope_band_copy(r).start()

    def slope_term():
        for r in others:
            slope_band_arrival(r).wait_recv()
        total = sl_band[0]
        for b in range(1, nb):
            total = total + sl_band[b]
        slope_out[...] = total[0:1, :nvars]
        line = lax.broadcasted_iota(jnp.int32, total.shape, 0)
        high, middle, low = three_way(total)
        slope_terms = jnp.where((line == 0) | (line == 3) | (line == 5), high, 0.0)
        slope_terms = jnp.where((line == 1) | (line == 4), middle, jnp.where(line == 2, low, slope_terms))
        line = lax.broadcasted_iota(jnp.int32, (8, cols), 0)
        for k in range(nc):
            high, middle, low = three_way(jnp.broadcast_to(mode_chain[k, 1:2, :], (8, cols)))
            mass_terms = jnp.where(line < 3, high, jnp.where(line < 5, middle, jnp.where(line == 5, low, 0.0)))
            outer[k] = lax.dot_general(slope_terms.astype(BF16), mass_terms.astype(BF16), (((0,), (0,)), ((), ())), preferred_element_type=F32)

    cap = got_ref.shape[2]
    ed = (got_ref.shape[1] - 8) // 2
    block = spread_ref.shape[0]
    lines = 128
    base = lax.broadcasted_iota(jnp.int32, (lines, cap), 0).astype(F32).astype(BF16)
    variable = lax.broadcasted_iota(jnp.int32, (nvars, cap), 0)
    matches = [(variable == got_ref[s, 2 * ed : 2 * ed + 1, :].astype(jnp.int32)).astype(F32).astype(BF16) for s in range(nc)]
    matches = jnp.concatenate(matches + matches, axis=1)

    def band_copy(to, source):
        return remote(rpart.at[:, at_band(to)], rslots.at[source], rq_send.at[to], rq_recv.at[source], me, to)

    per_block = block // cols

    def one_block(step, carry):
        n = lax.rem(step + 1 + band // per_block, width // block)

        def one_source(s, inner):
            values = got_ref[s, 0:ed, :]
            high = values.astype(BF16)
            low = (values - high.astype(F32)).astype(BF16)
            dofs = got_ref[s, ed : 2 * ed, :].astype(jnp.int32) - n * block
            for part_no in range(block // lines):
                shifted = dofs - part_no * lines
                shifted = jnp.where((shifted >= 0) & (shifted < lines), shifted, -1)
                place = shifted.astype(F32).astype(BF16)
                total_high = jnp.zeros((lines, cap), BF16)
                total_low = jnp.zeros((lines, cap), BF16)
                for i in range(ed):
                    hit = base == place[i : i + 1, :]
                    total_high = jnp.where(hit, high[i : i + 1, :], total_high)
                    total_low = jnp.where(hit, low[i : i + 1, :], total_low)
                at = pl.ds(pl.multiple_of(s * cap, cap), cap)
                spread_ref[part_no * lines : (part_no + 1) * lines, at] = total_high
                at = pl.ds(pl.multiple_of((s + nc) * cap, cap), cap)
                spread_ref[part_no * lines : (part_no + 1) * lines, at] = total_low
            return inner

        lax.fori_loop(0, nc, one_source, 0)
        at = pl.ds(pl.multiple_of(n * block, block), block)
        rpart[:, at] = lax.dot_general(matches, spread_ref[...], nt, preferred_element_type=F32)

        for j in range(per_block):
            to = n * per_block + j
            pl.when(to != band)(lambda to=to: band_copy(to, band).start())

        return carry

    lax.fori_loop(0, width // block, one_block, 0)

    slope_term()
    total = rpart[:, at_band(band)]
    for r in others:
        band_copy(band, band_from(r)).wait_recv()
        total = total + rslots[band_from(r)]
    rsum[...] = total

    def rhs_copy(to, source):
        return remote(rsum.at[at_group(to), :], rpiece.at[source], r_send.at[to], r_recv.at[source], to, band)

    for r in range(1, nc):
        rhs_copy(lax.rem(me + r, nc), me).start()
    rpiece[me] = rsum[at_group(me), :]

    def rhs_wait(k):
        pl.when(k != me)(lambda: rhs_copy(me, k).wait_recv())

    second_relays()

    def rs_copy(r):
        to = band_to(r)
        return remote(part.at[:, at_band(to)], slots.at[r], rs_send.at[r], rs_recv.at[r], me, to)

    def ag_copy(r):
        to = band_to(r)
        return remote(piece, full.at[:, at_band(band)], ag_send.at[r], ag_recv.at[r], me, to)

    def ag_arrival(r):
        source = band_from(r)
        return remote(piece, full.at[:, at_band(source)], ag_send.at[r], ag_recv.at[r], me, source)

    def reduce_start():
        for r in others:
            rs_copy(r).start()

    def reduce_end(own):
        total = own
        for r in reversed(others):
            rs_copy(r).wait_recv()
            total = total + slots[r]
        return total

    def reduce_sent():
        for r in others:
            rs_copy(r).wait_send()

    def gather_start(value):
        piece[...] = value
        for r in others:
            ag_copy(r).start()
        full[:, at_band(band)] = value

    def gather_end():
        for r in reversed(others):
            ag_arrival(r).wait_recv()

    def gather_sent():
        for r in others:
            ag_copy(r).wait_send()

    def block_wait(which, k):
        @pl.when((lax.rem(k, 2) != core) | (k == me))
        def _():
            pltpu.make_async_copy(blocks[which].at[k], blocks[which].at[k], mat.at[which, k]).wait()

    def split_diag(k):
        block_wait(0, k)
        high, low = split2(dbuf[k])
        dsplit[k, 0:cols, :] = high
        dsplit[k, cols : 2 * cols, :] = low

    def split_coup(k):
        block_wait(1, k)
        high, low = split2(cbuf[k])
        csplit[k, :, 0:cols] = high
        csplit[k, :, cols : 2 * cols] = low

    def narrow(value, weights, dims):
        wide = lax.dot_general(stacked_rows(value), weights, dims, preferred_element_type=F32)
        return (wide[:rows, :cols] + wide[:rows, cols:]) + (wide[rows:, :cols] + wide[rows:, cols:])

    def spread(value, weights, dims):
        both = stacked_rows(value)
        both = jnp.concatenate([both, both], axis=1)
        wide = lax.dot_general(both, weights, dims, preferred_element_type=F32)
        return wide[:rows] + wide[rows:]

    rhs_wait(0)
    gather_start(rpiece[0] + outer[0, at_group(me), :])
    relay_farthest(0, 0)
    relay_farthest(1, 1)
    relay_farthest(0, 1)
    split_diag(0)

    def forward(k, carry):
        pl.when(k > 0)(reduce_sent)
        split_coup(k + 1)
        gather_end()
        solved = narrow(full[...], dsplit[k], nt)
        part[...] = -spread(solved, csplit[k + 1], nt)
        reduce_start()
        ybuf[k] = solved
        gather_sent()
        rhs_wait(k + 1)
        relay_farthest(1, k + 2)
        relay_farthest(0, k + 2)
        split_diag(k + 1)
        gather_start(reduce_end(part[:, at_band(band)] + (rpiece[k + 1] + outer[k + 1, at_group(me), :])))
        return carry

    lax.fori_loop(0, nc - 1, forward, 0)
    reduce_sent()
    gather_end()
    ybuf[nc - 1] = narrow(full[...], dsplit[nc - 1], nt)

    def out_copy(k, source):
        return remote(xbuf.at[k], out_ref.at[at_group(source), :], out_send.at[k], out_recv.at[source], k, band)

    def backward(step, coupled):
        k = nc - 1 - step
        part[...] = spread(ybuf[k] - coupled, dsplit[k], nn)
        reduce_start()
        gather_sent()
        total = reduce_end(part[:, at_band(band)])
        gather_start(total)
        reduce_sent()
        xbuf[k] = total

        @pl.when(k != me)
        def _():
            out_copy(k, me).start()

        @pl.when(k == me)
        def _():
            out_ref[at_group(me), :] = total

        gather_end()
        return narrow(full[...], csplit[k], nn)

    coupled = lax.fori_loop(0, nc - 1, backward, jnp.zeros((rows, cols), F32))
    part[...] = spread(ybuf[0] - coupled, dsplit[0], nn)
    reduce_start()
    gather_sent()
    total = reduce_end(part[:, at_band(band)])
    xbuf[0] = total
    pl.when(me != 0)(lambda: out_copy(0, me).start())

    @pl.when(me == 0)
    def _():
        out_ref[at_group(0), :] = total

    for r in range(1, nc):
        other = lax.rem(me + r, nc)
        out_copy(other, me).wait_send()
        out_copy(me, other).wait_recv()
        rhs_copy(other, me).wait_send()
        slope_chain_copy(other, me).wait_send()
        mode_chain_copy(other, me).wait_send()
        element_copy(other, me).wait_send()
    reduce_sent()
    for r in range(1, nb):
        slope_band_copy(r).wait_send()
        mode_band_copy(r).wait_send()
        band_copy(band_to(r), band).wait_send()

    def sent(which):
        for i in range(3):
            own_copy(which, i).wait_send()

    for which in range(2):
        each_block(which, functools.partial(sent, which))
        for by in (1, 2, 3):

            def relayed(which=which, by=by):
                relay_on(which, by).wait_send()
                if by != 2:
                    pl.when(forwards(by))(lambda: relay_further(which, by).wait_send())

            each_relayed(which, by, relayed)


def on_device(nc, nb, diag_inverse, coupling, elem_stiff, elem_mass, elem_dofs, elem_slab, elem_var, mode, mass_mode, eigenvalue):
    band = lax.axis_index("band")
    cols, width = diag_inverse.shape
    ed, count = elem_dofs.shape
    cap = count // 4
    rows = VARS // nc
    padded = 256
    vmem = pl.BlockSpec(memory_space=pltpu.VMEM)
    anywhere = pl.BlockSpec(memory_space=pl.ANY)
    own_mass = lax.dynamic_slice_in_dim(mass_mode, band * cols, cols)[None, :]
    dma = pltpu.SemaphoreType.DMA
    eigvec_slope, eigval_slope = pl.pallas_call(
        functools.partial(solve_kernel, nc, nb),
        out_shape=(jax.ShapeDtypeStruct((VARS, cols), F32), jax.ShapeDtypeStruct((1, VARS), F32)),
        in_specs=[pl.BlockSpec(memory_space=pltpu.SMEM)] + [anywhere] * 9,
        out_specs=(vmem, vmem),
        scratch_shapes=[
            pltpu.VMEM((ed, count), jnp.int32),
            pltpu.VMEM((1, count), jnp.int32),
            pltpu.VMEM((1, count), jnp.int32),
            pltpu.VMEM((1, cols), F32),
            pltpu.VMEM((1, cols), F32),
            pltpu.VMEM((ed, ed, count), F32),
            pltpu.VMEM((ed, ed, count), F32),
            pltpu.VMEM((8, cols), F32),
            pltpu.VMEM((nc, 8, cols), F32),
            pltpu.VMEM((nc, cols), F32),
            pltpu.VMEM((nc * nb, cols), F32),
            pltpu.VMEM((ed, count), F32),
            pltpu.VMEM((ed, count), F32),
            pltpu.VMEM((nc, 2 * ed + 8, cap), F32),
            pltpu.VMEM((nc, 2 * ed + 8, cap), F32),
            pltpu.VMEM((8, padded), F32),
            pltpu.VMEM((nc, cols, width), F32),
            pltpu.VMEM((nc, width, cols), F32),
            pltpu.VMEM((nc, 2 * cols, width), BF16),
            pltpu.VMEM((nc, width, 2 * cols), BF16),
            pltpu.VMEM((256, 2 * nc * cap), BF16),
            pltpu.VMEM((VARS, width), F32),
            pltpu.VMEM((nb, VARS, cols), F32),
            pltpu.VMEM((VARS, cols), F32),
            pltpu.VMEM((nc, rows, cols), F32),
            pltpu.VMEM((nc, 8, padded), F32),
            pltpu.VMEM((nb, 8, padded), F32),
            pltpu.VMEM((nc, padded, cols), F32),
            pltpu.VMEM((rows, width), F32),
            pltpu.VMEM((nb, rows, cols), F32),
            pltpu.VMEM((rows, cols), F32),
            pltpu.VMEM((rows, width), F32),
            pltpu.VMEM((nc, rows, cols), F32),
            pltpu.VMEM((nc, rows, cols), F32),
            dma((7,)), dma((nc,)), dma((nc,)), dma((nb,)), dma((nb,)), dma((nc,)), dma((nc,)),
            dma((2, nc)), dma((2, 3)), dma((2, 4, 2)),
            dma((nc,)), dma((nc,)), dma((nb,)), dma((nb,)), dma((nc,)), dma((nc,)),
            dma((nb,)), dma((nb,)),
            dma((nb,)), dma((nb,)), dma((nb,)), dma((nb,)), dma((nc,)), dma((nc,)),
        ],
        compiler_params=pltpu.CompilerParams(collective_id=0, has_side_effects=True, vmem_limit_bytes=52 * 1024 * 1024),
        cost_estimate=pl.CostEstimate(flops=10**10, bytes_accessed=10**8, transcendentals=0),
        name="solve",
    )(eigenvalue, diag_inverse, coupling, elem_stiff, elem_mass, elem_dofs, elem_slab.reshape(1, count),
      elem_var.reshape(1, count), mode[None, :], own_mass)
    return eigvec_slope, eigval_slope.reshape(VARS)


def solution(mesh):
    nc, nb = mesh.shape["chain"], mesh.shape["band"]
    in_specs = (
        P(("chain", "band"), None),
        P("chain", "band"),
        P(None, None, ("chain", "band")),
        P(None, None, ("chain", "band")),
        P(None, ("chain", "band")),
        P(("chain", "band"), None),
        P(("chain", "band")),
        P(("chain", "band")),
        P("chain"),
        P(),
    )
    out_specs = (P(None, ("chain", "band")), P())
    return jax.shard_map(functools.partial(on_device, nc, nb), mesh=mesh, in_specs=in_specs, out_specs=out_specs, check_vma=False)
```
